256 devices in a mesh: dp: 16 (over z, core), seq: 16 (over x, y).
Axes of the slice: x: 4, y: 4, z: 8, core: 2. Of those that a mesh axis runs over, the one named last changes fastest.
Arguments:
- query_rows: bfloat16 [16, 2048, 2048], P('dp', 'seq'), may hold values from -16 to 16
- key_rows: bfloat16 [16, 2048, 2048], P('dp', 'seq'), may hold values from -16 to 16
- value_rows: bfloat16 [16, 2048, 2048], P('dp', 'seq'), may hold values from -6 to 6
- out_cotangent: bfloat16 [16, 2048, 2048], P('dp', 'seq'), may hold values from -6 to 6
- segment_ids: int32 [16, 2048], P('dp'), may hold values from 0 to 7, never falling along the last dimension, each value on 1 to 1536 neighbouring positions
- gain_query: float32 [16, 128], P('seq'), may hold values from 0.5 to 6
- gain_key: float32 [16, 128], P('seq'), may hold values from 0.5 to 6
Outputs:
- attended: bfloat16 [16, 2048, 2048], P('dp', 'seq')
- grad_query: bfloat16 [16, 2048, 2048], P('dp', 'seq')
- grad_key: bfloat16 [16, 2048, 2048], P('dp', 'seq')
- grad_value: bfloat16 [16, 2048, 2048], P('dp', 'seq')
- grad_gain_query: float32 [16, 128], P('seq')
- grad_gain_key: float32 [16, 128], P('seq')
The draws below stay inside these ranges and needn't reach their ends.
Inputs may be any that keep to these rules, and one draw needn't show every extreme that they name: `segment_ids`: image number of each token, never falling along the pack; each image with its prompt has 1 to 1536 tokens, one exactly 1536.
All inputs are finite; a program needn't handle non-finite values.
Results may differ from the reference program's by a relative error of at most 0.0065.
The reference program's roundings to bfloat16 on the way (of `weights_low` and `grad_scores`) count: a program that leaves them out, or rounds other values in their place, can miss the bound.
Values may be sent and summed in bfloat16 or wider, within the bound.
A program may use at most 64 MiB of HBM per device.

```python
import math
import jax
import jax.numpy as jnp
import numpy as np
from jax import lax

HD = 128
HEADS = 16
IMAGES = 8
PACK_LEN = 2048
PACKS = 16
MOST = 1536


def drawn_rows(key):
    return jnp.clip(jax.random.normal(key, (PACKS, PACK_LEN, HEADS * HD), jnp.float32), -6.0, 6.0)


def draw_query_rows(key, part):
    key = jax.random.fold_in(key, 11)
    rows = drawn_rows(key)
    return rows.astype(jnp.bfloat16)


def draw_key_rows(key, part):
    key = jax.random.fold_in(key, 23)
    rows = drawn_rows(key)
    return rows.astype(jnp.bfloat16)


def gain_table(key):
    values = jnp.exp(jax.random.uniform(key, (HEADS, HD), jnp.float32, math.log(0.5), math.log(2.0)))
    return values


def draw_gain_query(key, part):
    key = jax.random.fold_in(key, 31)
    return gain_table(key)


def draw_gain_key(key, part):
    key = jax.random.fold_in(key, 47)
    return gain_table(key)


def steps_of(own_key, shape, split, smallest, top_value):
    factor_of, own = 1.0, jax.random.fold_in(own_key, 6)
    for position, blocks in split:
        heights = jnp.exp(jax.random.uniform(jax.random.fold_in(own, position), (blocks,), jnp.float32, smallest / len(split), top_value / len(split)))
        factor_of = factor_of * jnp.repeat(heights, shape[position] // blocks).reshape([-1 if axis == position else 1 for axis in range(len(shape))])
    return factor_of


def profile(amount, total, reach, slope):
    loads = [(1 << 20) // math.isqrt(standing ** slope) + 1 for standing in range(2, amount + 1)]
    rest, given = total - reach - (amount - 1), [1] * (amount - 1)
    while rest > 0:
        candidates = [i for i in range(amount - 1) if given[i] < reach]
        whole, budget = sum([loads[i] for i in candidates]), rest
        for i in candidates:
            addition = min(reach - given[i], max(1, budget * loads[i] // whole), rest)
            given[i] = given[i] + addition
            rest = rest - addition
    return np.array([reach] + given)


def uneven(key, number_of, total, reach, lean):
    if number_of == 2:
        one = jax.random.randint(key, (), max(1, total - reach), min(reach, total - 1) + 1)
        return jnp.stack([one, total - one])
    sizes = jnp.asarray(profile(number_of, total, reach, lean), jnp.int32)
    twos = (number_of - 1) // 2
    source_of, sink = sizes[1:1 + 2 * twos:2], sizes[2:2 + 2 * twos:2]
    margin = jnp.minimum(source_of - 1, reach - sink)
    moved = jax.random.randint(jax.random.fold_in(key, 1), (twos,), 0, 1 << 20) % (margin + 1)
    sizes = sizes.at[1:1 + 2 * twos:2].set(source_of - moved).at[2:2 + 2 * twos:2].set(sink + moved)
    return sizes[jax.random.permutation(jax.random.fold_in(key, 2), number_of)]


def bell_draw(stream_key, extent, deviation, limit, shards=(), kind=jnp.bfloat16):
    result = jax.random.normal(stream_key, extent, jnp.float32) * deviation
    if len(shards) > 0:
        result = steps_of(stream_key, extent, shards, -0.22, 0.18) * result
    return jnp.clip(result, min=-limit, max=limit).astype(kind)


def setup_inputs(seed: int = 0) -> dict:
    key_of = jax.random.split(jax.random.key(seed), 8)
    query_rows = draw_query_rows(jax.random.fold_in(key_of[7], 71), 0)
    key_rows = draw_key_rows(jax.random.fold_in(key_of[7], 71), 0)
    value_rows = bell_draw(key_of[2], (PACKS, PACK_LEN, HEADS * HD), 1.0, 6.0, ((0, 16), (1, 16)))
    out_cotangent = bell_draw(key_of[3], (PACKS, PACK_LEN, HEADS * HD), 1.0, 6.0, ((0, 16), (1, 16)))
    segment_ids = jax.vmap(lambda own: jnp.searchsorted(jnp.cumsum(uneven(own, IMAGES, PACK_LEN, MOST, 2)), jnp.arange(PACK_LEN), side="right"))(jax.random.split(key_of[4], PACKS)).reshape((PACKS, PACK_LEN)).astype(jnp.int32)
    gain_query = draw_gain_query(jax.random.fold_in(key_of[7], 71), 0)
    gain_key = draw_gain_key(jax.random.fold_in(key_of[7], 71), 0)
    return dict(query_rows=query_rows, key_rows=key_rows, value_rows=value_rows, out_cotangent=out_cotangent, segment_ids=segment_ids, gain_query=gain_query, gain_key=gain_key)


NEGATIVE = -1e+30
EPSILON = 1e-06

def normalize(rows, gain):
    inverse = lax.rsqrt(lax.optimization_barrier(jnp.mean(rows * rows, axis=-1, keepdims=True)) + EPSILON)
    return rows * inverse * gain

def one_head(pieces):
    queries, keys_all, values_all, grads_out, segments, gain_row, gain_col = pieces
    score_scale = 1.0 / math.sqrt(HD)
    query_norm32, query_back = jax.vjp(normalize, queries.astype(jnp.float32), gain_row)
    key_norm32, key_back = jax.vjp(normalize, keys_all.astype(jnp.float32), gain_col)
    query_norm = query_norm32.astype(jnp.bfloat16)
    key_norm = key_norm32.astype(jnp.bfloat16)
    scores = jnp.dot(query_norm, key_norm.T, preferred_element_type=jnp.float32) * score_scale
    allowed = segments[:, None] == segments[None, :]
    row_max = lax.optimization_barrier(jnp.max(jnp.where(allowed, scores, NEGATIVE), axis=1))
    shifted = jnp.where(allowed, jnp.exp(scores - row_max[:, None]), 0.0)
    weights = shifted / lax.optimization_barrier(jnp.sum(shifted, axis=1))[:, None]
    weights_low = weights.astype(jnp.bfloat16)
    output_full = jnp.dot(weights_low, values_all, preferred_element_type=jnp.float32)
    attended = output_full.astype(jnp.bfloat16)
    grad_probs = jnp.dot(grads_out, values_all.T, preferred_element_type=jnp.float32)
    row_delta = lax.optimization_barrier(jnp.sum(grads_out.astype(jnp.float32) * output_full, axis=1))
    grad_scores = (weights * (grad_probs - row_delta[:, None])).astype(jnp.bfloat16)
    query_grad_norm = jnp.dot(grad_scores, key_norm, preferred_element_type=jnp.float32) * score_scale
    key_grad_norm = jnp.dot(grad_scores.T, query_norm, preferred_element_type=jnp.float32) * score_scale
    value_grad = jnp.dot(weights_low.T, grads_out, preferred_element_type=jnp.float32).astype(jnp.bfloat16)
    query_grad, gain_grad_q = query_back(query_grad_norm)
    key_grad, gain_grad_k = key_back(key_grad_norm)
    return (attended, query_grad.astype(jnp.bfloat16), key_grad.astype(jnp.bfloat16), value_grad, gain_grad_q, gain_grad_k)

def reference(query_rows, key_rows, value_rows, out_cotangent, segment_ids, gain_query, gain_key):

    def by_head(array):
        return array.reshape(PACKS, PACK_LEN, HEADS, HD).transpose(0, 2, 1, 3).reshape(PACKS * HEADS, PACK_LEN, HD)

    def by_token(array):
        return array.reshape(PACKS, HEADS, PACK_LEN, HD).transpose(0, 2, 1, 3).reshape(PACKS, PACK_LEN, HEADS * HD)
    seg_rows = jnp.broadcast_to(segment_ids[:, None, :], (PACKS, HEADS, PACK_LEN)).reshape(PACKS * HEADS, PACK_LEN)
    gains_q = jnp.broadcast_to(gain_query[None], (PACKS, HEADS, HD)).reshape(PACKS * HEADS, HD)
    gains_k = jnp.broadcast_to(gain_key[None], (PACKS, HEADS, HD)).reshape(PACKS * HEADS, HD)
    results = lax.map(one_head, (by_head(query_rows), by_head(key_rows), by_head(value_rows), by_head(out_cotangent), seg_rows, gains_q, gains_k))
    attended, query_grad, key_grad, value_grad, gain_grad_q, gain_grad_k = results
    return (by_token(attended), by_token(query_grad), by_token(key_grad), by_token(value_grad), lax.optimization_barrier(jnp.sum(gain_grad_q.reshape(PACKS, HEADS, HD), axis=0)), lax.optimization_barrier(jnp.sum(gain_grad_k.reshape(PACKS, HEADS, HD), axis=0)))
```

```python
import functools
import math

import jax
import jax.numpy as jnp
from jax import lax
from jax.experimental import pallas as pl
from jax.experimental.pallas import tpu as pltpu
from jax.sharding import PartitionSpec as P

MESH = pl.DeviceIdType.MESH
EPSILON = 1e-06
NEGATIVE = -1e30
HD = 128
LEN = 2048
BIG = 1536
REST = LEN - BIG
ROWS = 256
SIDE = 4
SHARDS = SIDE * SIDE
TOK = LEN // SHARDS
SCALE = 1.0 / math.sqrt(HD)
EXP2_SCALE = SCALE * math.log2(math.e)
F32 = jnp.float32
BF16 = jnp.bfloat16


def dot_nt(a, b):
    return lax.dot_general(a, b, (((1,), (1,)), ((), ())), preferred_element_type=F32)


def dot_nn(a, b):
    return jnp.dot(a, b, preferred_element_type=F32)


def rows_at(start, size):
    return pl.ds(pl.multiple_of(start, size), size)


def kernel(
    dp_size,
    q_in, k_in, v_in, g_in, seg_s, seg_v, gain_q, gain_k,
    o_out, dq_out, dk_out, dv_out, ggq_out, ggk_out,
    rx, tx, shifted, qr, kr, vr, gr, q_t, g_t, marks, w_big, w_rest,
    go, gq, gk, gv, dk_t, dv_t, gains, gain_rx,
    in_send, in_recv, in_local, out_send, out_recv, out_local, gain_send, gain_recv,
):
    d = lax.axis_index("dp")
    me = lax.axis_index("seq")
    mx, my = me // SIDE, me % SIDE
    rounds = dp_size.bit_length() - 1

    def peer(j):
        return (mx + j // SIDE) % SIDE * SIDE + (my + j % SIDE) % SIDE

    def partner(r):
        bit = 1 << r
        return d + bit - 2 * bit * ((d // bit) % 2)

    barrier = pltpu.get_barrier_semaphore()

    def greet(j, carry):
        pl.semaphore_signal(barrier, inc=1, device_id=(d, peer(j)), device_id_type=MESH)
        return carry

    lax.fori_loop(1, SHARDS, greet, 0)
    for r in range(rounds):
        pl.semaphore_signal(barrier, inc=1, device_id=(partner(r), me), device_id_type=MESH)
    pl.semaphore_wait(barrier, SHARDS - 1 + rounds)

    sources = (q_in, k_in, v_in, g_in)
    targets = (o_out, dq_out, dk_out, dv_out)
    for a in range(4):

        def send(j, carry, a=a):
            to = peer(j)
            pltpu.make_async_remote_copy(
                src_ref=sources[a].at[0, :, rows_at(to * HD, HD)],
                dst_ref=rx.at[a, rows_at(me * TOK, TOK)],
                send_sem=in_send.at[a],
                recv_sem=in_recv.at[a],
                device_id=(d, to),
                device_id_type=MESH,
            ).start()
            return carry

        lax.fori_loop(1, SHARDS, send, 0)
        pltpu.make_async_copy(
            sources[a].at[0, :, rows_at(me * HD, HD)], rx.at[a, rows_at(me * TOK, TOK)], in_local.at[a]
        ).start()

    def arrived(a):
        part = rx.at[a, pl.ds(0, LEN - TOK)]
        pltpu.make_async_copy(part, part, in_recv.at[a]).wait()
        own = rx.at[a, pl.ds(0, TOK)]
        pltpu.make_async_copy(own, own, in_local.at[a]).wait()

    image = seg_s[0, LEN // 2]

    def halve(_, held):
        low, high = held
        mid = (low + high) // 2
        inside = seg_s[0, mid] >= image
        return (jnp.where(inside, low, mid + 1), jnp.where(inside, mid, high))

    first, _ = lax.fori_loop(0, 10, halve, (jnp.int32(0), jnp.int32(REST)))

    lanes = lax.broadcasted_iota(jnp.int32, (TOK, HD), 1).astype(F32)
    for t in range(2 * REST // TOK):
        token = (BIG + t * TOK) % LEN
        numbers = seg_v[0:1, token : token + TOK].astype(F32)
        column = jnp.broadcast_to(numbers, (HD, TOK)).T
        shifted[t * TOK : (t + 1) * TOK] = jnp.where(column == lanes, 1.0, 0.0)
    marks[...] = shifted[pl.ds(first, REST), :].astype(BF16)

    def wrap():
        shifted[LEN : LEN + REST] = shifted[0:REST]

    def norm_parts(a, at):
        x = rx[a, at, :].astype(F32)
        inverse = lax.rsqrt(jnp.mean(x * x, axis=1, keepdims=True) + EPSILON)
        return x * inverse, inverse

    def fill(a, gain):

        def body(b, carry):
            at = rows_at(b * ROWS, ROWS)
            if gain is None:
                shifted[at, :] = rx[a, at, :].astype(F32)
            else:
                shifted[at, :] = norm_parts(a, at)[0] * gain[...]
            return carry

        lax.fori_loop(0, LEN // ROWS, body, 0)
        wrap()

    def roll_into(rolled, turned):

        def body(b, carry):
            value = shifted[pl.ds(first + b * ROWS, ROWS), :]
            rolled[rows_at(b * ROWS, ROWS), :] = value.astype(BF16)
            if turned is not None:
                turned[:, rows_at(b * ROWS, ROWS)] = value.T.astype(BF16)
            return carry

        lax.fori_loop(0, LEN // ROWS, body, 0)

    arrived(0)
    fill(0, gain_q)
    roll_into(qr, q_t)
    arrived(1)
    fill(1, gain_k)
    roll_into(kr, None)

    def weights_of(scores):
        top = jnp.max(scores, axis=1, keepdims=True)
        powers = jnp.exp2((scores - top) * EXP2_SCALE)
        return powers * (1.0 / jnp.sum(powers, axis=1, keepdims=True))

    def big_weights(b, carry):
        at = rows_at(b * ROWS, ROWS)
        w_big[at, :] = weights_of(dot_nt(qr[at, :], kr[0:BIG, :]))
        return carry

    lax.fori_loop(0, BIG // ROWS, big_weights, 0)

    def rest_weights(b, carry):
        at = rows_at(b * ROWS, ROWS)
        scores = dot_nt(qr[rows_at(BIG + b * ROWS, ROWS), :], kr[BIG:LEN, :])
        allowed = dot_nt(marks[at, :], marks[...]) > 0.5
        w_rest[at, :] = weights_of(jnp.where(allowed, scores, NEGATIVE))
        return carry

    lax.fori_loop(0, REST // ROWS, rest_weights, 0)

    arrived(2)
    fill(2, None)
    roll_into(vr, None)

    def big_values(b, carry):
        at = rows_at(b * ROWS, ROWS)
        go[rows_at(REST + b * ROWS, ROWS), :] = dot_nn(w_big[at, :].astype(BF16), vr[0:BIG, :])
        return carry

    lax.fori_loop(0, BIG // ROWS, big_values, 0)

    def rest_values(b, carry):
        at = rows_at(b * ROWS, ROWS)
        value = dot_nn(w_rest[at, :].astype(BF16), vr[BIG:LEN, :])
        go[rows_at(LEN + b * ROWS, ROWS), :] = value
        go[at, :] = value
        return carry

    lax.fori_loop(0, REST // ROWS, rest_values, 0)

    def send_back(a, t):
        @pl.when(t != me)
        def _():
            pltpu.make_async_remote_copy(
                src_ref=tx.at[a, rows_at(t * TOK, TOK)],
                dst_ref=targets[a].at[0, :, rows_at(me * HD, HD)],
                send_sem=out_send.at[a],
                recv_sem=out_recv.at[a],
                device_id=(d, t),
                device_id_type=MESH,
            ).start()

        @pl.when(t == me)
        def _():
            pltpu.make_async_copy(
                tx.at[a, rows_at(t * TOK, TOK)], targets[a].at[0, :, rows_at(me * HD, HD)], out_local.at[a]
            ).start()

    def token_rows(ref, t):
        return ref[pl.ds(REST - first + t * TOK, TOK), :]

    def send_plain(a, ref):

        def body(j, carry):
            t = peer(j)
            tx[a, rows_at(t * TOK, TOK), :] = token_rows(ref, t).astype(BF16)
            send_back(a, t)
            return carry

        lax.fori_loop(0, SHARDS, body, 0)

    send_plain(0, go)

    arrived(3)
    fill(3, None)
    roll_into(gr, g_t)
    dk_t[...] = jnp.zeros_like(dk_t)
    dv_t[...] = jnp.zeros_like(dv_t)

    def backward(weights, queries_at, keys_at, out_at):
        low = weights.astype(BF16)
        grads = gr[queries_at, :]
        delta = jnp.sum(grads.astype(F32) * go[out_at, :], axis=1, keepdims=True)
        grad_probs = dot_nt(grads, vr[keys_at, :])
        grad_scores = (weights * (grad_probs - delta)).astype(BF16)
        gq[out_at, :] = dot_nn(grad_scores, kr[keys_at, :]) * SCALE
        dk_t[:, keys_at] += dot_nn(q_t[:, queries_at], grad_scores)
        dv_t[:, keys_at] += dot_nn(g_t[:, queries_at], low)

    def rest_backward(b, carry):
        backward(
            w_rest[rows_at(b * ROWS, ROWS), :],
            rows_at(BIG + b * ROWS, ROWS),
            pl.ds(BIG, REST),
            rows_at(LEN + b * ROWS, ROWS),
        )
        return carry

    lax.fori_loop(0, REST // ROWS, rest_backward, 0)

    def big_backward(b, carry):
        at = rows_at(b * ROWS, ROWS)
        backward(w_big[at, :], at, pl.ds(0, BIG), rows_at(REST + b * ROWS, ROWS))
        return carry

    lax.fori_loop(0, BIG // ROWS, big_backward, 0)

    def head(ref):
        ref[0:REST] = ref[LEN : LEN + REST]

    def turn_back(ref, turned, factor):

        def body(b, carry):
            value = turned[:, rows_at(b * ROWS, ROWS)].T
            ref[rows_at(REST + b * ROWS, ROWS), :] = value if factor is None else value * factor
            return carry

        lax.fori_loop(0, LEN // ROWS, body, 0)
        head(ref)

    def send_normed(a, source, ref, gain):

        def body(j, total):
            t = peer(j)
            unit, inverse = norm_parts(source, rows_at(t * TOK, TOK))
            grad = token_rows(ref, t)
            total = total + jnp.sum(grad * unit, axis=0, keepdims=True)
            scaled = grad * gain[...]
            inner = jnp.mean(scaled * unit, axis=1, keepdims=True)
            tx[a, rows_at(t * TOK, TOK), :] = (inverse * (scaled - unit * inner)).astype(BF16)
            send_back(a, t)
            return total

        return lax.fori_loop(0, SHARDS, body, jnp.zeros((1, HD), F32))

    gains[0] = jnp.zeros((8, HD), F32)
    head(gq)
    gains[0, 0:1, :] = send_normed(1, 0, gq, gain_q)
    turn_back(gk, dk_t, SCALE)
    gains[0, 1:2, :] = send_normed(2, 1, gk, gain_k)
    turn_back(gv, dv_t, None)
    send_plain(3, gv)

    for r in range(rounds):
        copy = pltpu.make_async_remote_copy(
            src_ref=gains.at[r],
            dst_ref=gain_rx.at[r],
            send_sem=gain_send.at[r],
            recv_sem=gain_recv.at[r],
            device_id=(partner(r), me),
            device_id_type=MESH,
        )
        copy.start()
        copy.wait()
        gains[r + 1] = gains[r] + gain_rx[r]
    ggq_out[...] = gains[rounds, 0:1, :]
    ggk_out[...] = gains[rounds, 1:2, :]

    for a in range(4):
        part = rx.at[a, pl.ds(0, LEN - TOK)]
        pltpu.make_async_copy(part, part, in_send.at[a]).wait()
        pltpu.make_async_copy(part, part, out_send.at[a]).wait()
        own = rx.at[a, pl.ds(0, TOK)]
        pltpu.make_async_copy(own, own, out_local.at[a]).wait()
        landed = targets[a].at[0, :, pl.ds(0, LEN - TOK)]
        pltpu.make_async_copy(landed, landed, out_recv.at[a]).wait()


def on_device(dp_size, query_rows, key_rows, value_rows, out_cotangent, segment_ids, gain_query, gain_key):
    rounds = dp_size.bit_length() - 1
    rows = jax.ShapeDtypeStruct((1, TOK, LEN), BF16)
    gain = jax.ShapeDtypeStruct((1, HD), F32)
    hbm = pl.BlockSpec(memory_space=pl.ANY)
    vmem = pl.BlockSpec(memory_space=pltpu.VMEM)
    smem = pl.BlockSpec(memory_space=pltpu.SMEM)
    dma = pltpu.SemaphoreType.DMA
    return pl.pallas_call(
        functools.partial(kernel, dp_size),
        out_shape=(rows, rows, rows, rows, gain, gain),
        in_specs=[hbm, hbm, hbm, hbm, smem, vmem, vmem, vmem],
        out_specs=(hbm, hbm, hbm, hbm, vmem, vmem),
        scratch_shapes=[
            pltpu.VMEM((4, LEN, HD), BF16),
            pltpu.VMEM((4, LEN, HD), BF16),
            pltpu.VMEM((LEN + REST, HD), F32),
            pltpu.VMEM((LEN, HD), BF16),
            pltpu.VMEM((LEN, HD), BF16),
            pltpu.VMEM((LEN, HD), BF16),
            pltpu.VMEM((LEN, HD), BF16),
            pltpu.VMEM((HD, LEN), BF16),
            pltpu.VMEM((HD, LEN), BF16),
            pltpu.VMEM((REST, HD), BF16),
            pltpu.VMEM((BIG, BIG), F32),
            pltpu.VMEM((REST, REST), F32),
            pltpu.VMEM((LEN + REST, HD), F32),
            pltpu.VMEM((LEN + REST, HD), F32),
            pltpu.VMEM((LEN + REST, HD), F32),
            pltpu.VMEM((LEN + REST, HD), F32),
            pltpu.VMEM((HD, LEN), F32),
            pltpu.VMEM((HD, LEN), F32),
            pltpu.VMEM((rounds + 1, 8, HD), F32),
            pltpu.VMEM((rounds + 1, 8, HD), F32),
            dma((4,)), dma((4,)), dma((4,)), dma((4,)), dma((4,)), dma((4,)),
            dma((rounds + 1,)), dma((rounds + 1,)),
        ],
        compiler_params=pltpu.CompilerParams(
            collective_id=0, has_side_effects=True, vmem_limit_bytes=56 * 2**20
        ),
    )(query_rows, key_rows, value_rows, out_cotangent, segment_ids, segment_ids, gain_query, gain_key)


def solution(mesh):
    placed = (
        P("dp", "seq", None),
        P("dp", "seq", None),
        P("dp", "seq", None),
        P("dp", "seq", None),
        P("dp", None),
        P("seq", None),
        P("seq", None),
    )
    return jax.shard_map(
        functools.partial(on_device, mesh.shape["dp"]),
        mesh=mesh,
        in_specs=placed,
        out_specs=(
            P("dp", "seq", None),
            P("dp", "seq", None),
            P("dp", "seq", None),
            P("dp", "seq", None),
            P("seq", None),
            P("seq", None),
        ),
        check_vma=False,
    )
```

```python
import functools
import math

import jax
import jax.numpy as jnp
from jax import lax
from jax.experimental import pallas as pl
from jax.experimental.pallas import tpu as pltpu
from jax.sharding import PartitionSpec as P

MESH = pl.DeviceIdType.MESH
EPSILON = 1e-06
NEGATIVE = -1e30
HD = 128
LEN = 2048
BIG = 1536
REST = LEN - BIG
ROWS = 256
SIDE = 4
SHARDS = SIDE * SIDE
TOK = LEN // SHARDS
GROUP = TOK * SIDE
SCALE = 1.0 / math.sqrt(HD)
EXP2_SCALE = SCALE * math.log2(math.e)
F32 = jnp.float32
BF16 = jnp.bfloat16


def dot_nt(a, b):
    return lax.dot_general(a, b, (((1,), (1,)), ((), ())), preferred_element_type=F32)


def dot_nn(a, b):
    return jnp.dot(a, b, preferred_element_type=F32)


def rows_at(start, size):
    return pl.ds(pl.multiple_of(start, size), size)


def kernel(
    dp_size,
    q_in, k_in, v_in, g_in, seg_in, gain_q_in, gain_k_in,
    o_out, dq_out, dk_out, dv_out, ggq_out, ggk_out,
    seg_s, seg_v, gain_q, gain_k, rx, tx, shifted, units, inverses, qr, kr, vr, gr, q_t, g_t, marks, p_big, p_rest, scale_of,
    go, gq, gk, gv, dk_t, dv_t, gains, gain_rx,
    in_send, in_recv, in_local, out_send, out_recv, out_local, gain_send, gain_recv, ready, small,
):
    d = lax.axis_index("dp")
    me = lax.axis_index("seq")
    mx, my = me // SIDE, me % SIDE
    rounds = dp_size.bit_length() - 1

    def peer(j):
        return (mx + j // SIDE) % SIDE * SIDE + (my + j % SIDE) % SIDE

    def upper(r):
        return (d // (1 << r)) % 2

    def partner(r):
        return d + (1 << r) - 2 * (1 << r) * upper(r)

    barrier = pltpu.get_barrier_semaphore()

    def greet(j, carry):
        pl.semaphore_signal(barrier, inc=1, device_id=(d, peer(j)), device_id_type=MESH)
        return carry

    for r in range(rounds):

        @pl.when(upper(r) == 0)
        def _(r=r):
            pl.semaphore_signal(barrier, inc=1, device_id=(partner(r), me), device_id_type=MESH)

    lax.fori_loop(1, SHARDS, greet, 0)
    pl.semaphore_wait(barrier, SHARDS - 1 + sum(upper(r) for r in range(rounds)))

    sources = (q_in, k_in, v_in, g_in)
    targets = (o_out, dq_out, dk_out, dv_out)
    for a in range(4):

        def send(j, carry, a=a):
            to = peer(j)
            pltpu.make_async_remote_copy(
                src_ref=sources[a].at[0, :, rows_at(to * HD, HD)],
                dst_ref=rx.at[a, rows_at(me * TOK, TOK)],
                send_sem=in_send.at[a],
                recv_sem=in_recv.at[a],
                device_id=(d, to),
                device_id_type=MESH,
            ).start()
            return carry

        lax.fori_loop(1, SHARDS, send, 0)
        pltpu.make_async_copy(
            sources[a].at[0, :, rows_at(me * HD, HD)], rx.at[a, rows_at(me * TOK, TOK)], in_local.at[a]
        ).start()

    for r in range(rounds):

        @pl.when(upper(r) == 1)
        def _(r=r):
            pl.semaphore_signal(ready.at[r], inc=1, device_id=(partner(r), me), device_id_type=MESH)

    fetches = [
        pltpu.make_async_copy(here, there, small.at[i])
        for i, (here, there) in enumerate(
            ((seg_in, seg_s), (seg_in, seg_v), (gain_q_in, gain_q), (gain_k_in, gain_k))
        )
    ]
    for fetch in fetches:
        fetch.start()
    for fetch in fetches:
        fetch.wait()

    image = seg_s[0, LEN // 2]

    def halve(_, held):
        low, high = held
        mid = (low + high) // 2
        inside = seg_s[0, mid] >= image
        return (jnp.where(inside, low, mid + 1), jnp.where(inside, mid, high))

    first, _ = lax.fori_loop(0, 10, halve, (jnp.int32(0), jnp.int32(REST)))

    lanes = lax.broadcasted_iota(jnp.int32, (TOK, HD), 1).astype(F32)
    for t in range(2 * REST // TOK):
        token = (BIG + t * TOK) % LEN
        numbers = seg_v[0:1, token : token + TOK].astype(F32)
        column = jnp.broadcast_to(numbers, (HD, TOK)).T
        shifted[t * TOK : (t + 1) * TOK] = jnp.where(column == lanes, 1.0, 0.0)
    marks[...] = shifted[pl.ds(first, REST), :].astype(BF16)
    dk_t[...] = jnp.zeros_like(dk_t)
    dv_t[...] = jnp.zeros_like(dv_t)
    gains[0] = jnp.zeros((8, HD), F32)

    def fill(a, gain):
        part = rx.at[a, pl.ds(0, LEN - TOK)]
        pltpu.make_async_copy(part, part, in_recv.at[a]).wait()
        own = rx.at[a, pl.ds(0, TOK)]
        pltpu.make_async_copy(own, own, in_local.at[a]).wait()
        for g in range(SIDE):
            at = pl.ds(g * GROUP, GROUP)
            x = rx[a, at, :].astype(F32)
            if gain is not None:
                inverse = lax.rsqrt(jnp.mean(x * x, axis=1, keepdims=True) + EPSILON)
                x = x * inverse
                units[a, at, :] = x
                inverses[a, at, :] = jnp.broadcast_to(inverse, (GROUP, HD))
                x = x * gain[...]
            shifted[at, :] = x
        shifted[LEN : LEN + REST] = shifted[0:REST]

    def roll_into(rolled, turned):

        def body(b, carry):
            value = shifted[pl.ds(first + b * GROUP, GROUP), :]
            rolled[rows_at(b * GROUP, GROUP), :] = value.astype(BF16)
            if turned is not None:
                turned[:, rows_at(b * GROUP, GROUP)] = value.T.astype(BF16)
            return carry

        lax.fori_loop(0, LEN // GROUP, body, 0)

    fill(0, gain_q)
    roll_into(qr, q_t)
    fill(1, gain_k)
    roll_into(kr, None)

    def powers_of(scores, at):
        top = jnp.max(scores, axis=1, keepdims=True)
        powers = jnp.exp2((scores - top) * EXP2_SCALE)
        scale_of[at, :] = jnp.broadcast_to(1.0 / jnp.sum(powers, axis=1, keepdims=True), (ROWS, HD))
        return powers

    def big_powers(b, carry):
        at = rows_at(b * ROWS, ROWS)
        p_big[at, :] = powers_of(dot_nt(qr[at, :], kr[0:BIG, :]), at)
        return carry

    lax.fori_loop(0, BIG // ROWS, big_powers, 0)

    def rest_powers(b, carry):
        at = rows_at(b * ROWS, ROWS)
        rolled_at = rows_at(BIG + b * ROWS, ROWS)
        scores = dot_nt(qr[rolled_at, :], kr[BIG:LEN, :])
        allowed = dot_nt(marks[at, :], marks[...]) > 0.5
        p_rest[at, :] = powers_of(jnp.where(allowed, scores, NEGATIVE), rolled_at)
        return carry

    lax.fori_loop(0, REST // ROWS, rest_powers, 0)

    fill(2, None)
    roll_into(vr, None)

    def big_values(b, carry):
        at = rows_at(b * ROWS, ROWS)
        low = (p_big[at, :] * scale_of[at, 0:1]).astype(BF16)
        go[rows_at(REST + b * ROWS, ROWS), :] = dot_nn(low, vr[0:BIG, :])
        return carry

    lax.fori_loop(0, BIG // ROWS, big_values, 0)

    def rest_values(b, carry):
        at = rows_at(b * ROWS, ROWS)
        low = (p_rest[at, :] * scale_of[rows_at(BIG + b * ROWS, ROWS), 0:1]).astype(BF16)
        value = dot_nn(low, vr[BIG:LEN, :])
        go[rows_at(LEN + b * ROWS, ROWS), :] = value
        go[at, :] = value
        return carry

    lax.fori_loop(0, REST // ROWS, rest_values, 0)

    def send_back(a):
        target = targets[a].at[0, :, rows_at(me * HD, HD)]

        def send(j, carry):
            to = peer(j)
            pltpu.make_async_remote_copy(
                src_ref=tx.at[a, rows_at(to * TOK, TOK)],
                dst_ref=target,
                send_sem=out_send.at[a],
                recv_sem=out_recv.at[a],
                device_id=(d, to),
                device_id_type=MESH,
            ).start()
            return carry

        lax.fori_loop(1, SHARDS, send, 0)
        pltpu.make_async_copy(tx.at[a, rows_at(me * TOK, TOK)], target, out_local.at[a]).start()

    def token_group(ref, g):
        return ref[pl.ds(REST - first + g * GROUP, GROUP), :]

    def send_plain(a, ref):
        for g in range(SIDE):
            tx[a, g * GROUP : (g + 1) * GROUP, :] = token_group(ref, g).astype(BF16)
        send_back(a)

    send_plain(0, go)

    fill(3, None)
    roll_into(gr, g_t)

    def backward(powers, queries_at, keys_at, out_at):
        weights = powers * scale_of[queries_at, 0:1]
        low = weights.astype(BF16)
        grads = gr[queries_at, :]
        delta = jnp.sum(grads.astype(F32) * go[out_at, :], axis=1, keepdims=True)
        grad_probs = dot_nt(grads, vr[keys_at, :])
        grad_scores = (weights * (grad_probs - delta)).astype(BF16)
        gq[out_at, :] = dot_nn(grad_scores, kr[keys_at, :]) * SCALE
        dk_t[:, keys_at] += dot_nn(q_t[:, queries_at], grad_scores)
        dv_t[:, keys_at] += dot_nn(g_t[:, queries_at], low)

    def rest_backward(b, carry):
        backward(
            p_rest[rows_at(b * ROWS, ROWS), :],
            rows_at(BIG + b * ROWS, ROWS),
            pl.ds(BIG, REST),
            rows_at(LEN + b * ROWS, ROWS),
        )
        return carry

    lax.fori_loop(0, REST // ROWS, rest_backward, 0)

    def big_backward(b, carry):
        at = rows_at(b * ROWS, ROWS)
        backward(p_big[at, :], at, pl.ds(0, BIG), rows_at(REST + b * ROWS, ROWS))
        return carry

    lax.fori_loop(0, BIG // ROWS, big_backward, 0)

    def head(ref):
        ref[0:REST] = ref[LEN : LEN + REST]

    def turn_back(ref, turned, factor):

        def body(b, carry):
            value = turned[:, rows_at(b * GROUP, GROUP)].T
            ref[rows_at(REST + b * GROUP, GROUP), :] = value if factor is None else value * factor
            return carry

        lax.fori_loop(0, LEN // GROUP, body, 0)
        head(ref)

    def send_normed(a, source, ref, gain):
        total = jnp.zeros((1, HD), F32)
        for g in range(SIDE):
            at = pl.ds(g * GROUP, GROUP)
            unit = units[source, at, :]
            grad = token_group(ref, g)
            total = total + jnp.sum(grad * unit, axis=0, keepdims=True)
            scaled = grad * gain[...]
            inner = jnp.mean(scaled * unit, axis=1, keepdims=True)
            tx[a, at, :] = (inverses[source, at, :] * (scaled - unit * inner)).astype(BF16)
        send_back(a)
        return total

    head(gq)
    gains[0, 0:1, :] = send_normed(1, 0, gq, gain_q)
    turn_back(gk, dk_t, SCALE)
    gains[0, 1:2, :] = send_normed(2, 1, gk, gain_k)
    turn_back(gv, dv_t, None)
    send_plain(3, gv)

    for r in range(rounds):

        @pl.when(upper(r) == 0)
        def _(r=r):
            pl.semaphore_wait(ready.at[r], 1)

        copy = pltpu.make_async_remote_copy(
            src_ref=gains.at[r],
            dst_ref=gain_rx.at[r],
            send_sem=gain_send.at[r],
            recv_sem=gain_recv.at[r],
            device_id=(partner(r), me),
            device_id_type=MESH,
        )
        copy.start()
        copy.wait()
        gains[r + 1] = gains[r] + gain_rx[r]
    ggq_out[...] = gains[rounds, 0:1, :]
    ggk_out[...] = gains[rounds, 1:2, :]

    for a in range(4):
        part = rx.at[a, pl.ds(0, LEN - TOK)]
        pltpu.make_async_copy(part, part, in_send.at[a]).wait()
        pltpu.make_async_copy(part, part, out_send.at[a]).wait()
        own = rx.at[a, pl.ds(0, TOK)]
        pltpu.make_async_copy(own, own, out_local.at[a]).wait()
        landed = targets[a].at[0, :, pl.ds(0, LEN - TOK)]
        pltpu.make_async_copy(landed, landed, out_recv.at[a]).wait()


def settle(*refs):
    held, placed, sem = refs[:6], refs[6:12], refs[12]
    copies = [pltpu.make_async_copy(held[i], placed[i], sem.at[i]) for i in range(6)]
    for copy in copies:
        copy.start()
    for copy in copies:
        copy.wait()


def on_device(dp_size, *operands):
    rounds = dp_size.bit_length() - 1
    rows = jax.ShapeDtypeStruct((1, TOK, LEN), BF16)
    gain = jax.ShapeDtypeStruct((1, HD), F32)
    hbm = pl.BlockSpec(memory_space=pltpu.HBM)
    vmem = pl.BlockSpec(memory_space=pltpu.VMEM)
    place = pl.BlockSpec(memory_space=pl.ANY)
    dma = pltpu.SemaphoreType.DMA
    spread = pltpu.VMEM((LEN + REST, HD), F32)
    packed = pltpu.VMEM((LEN, HD), BF16)
    results = pl.pallas_call(
        functools.partial(kernel, dp_size),
        out_shape=(rows, rows, rows, rows, gain, gain),
        in_specs=[hbm] * 7,
        out_specs=(place, place, place, place, vmem, vmem),
        scratch_shapes=[
            pltpu.SMEM((1, LEN), jnp.int32),
            pltpu.VMEM((1, LEN), jnp.int32),
            pltpu.VMEM((1, HD), F32),
            pltpu.VMEM((1, HD), F32),
            pltpu.VMEM((4, LEN, HD), BF16),
            pltpu.VMEM((4, LEN, HD), BF16),
            spread,
            pltpu.VMEM((2, LEN, HD), F32),
            pltpu.VMEM((2, LEN, HD), F32),
            packed, packed, packed, packed,
            pltpu.VMEM((HD, LEN), BF16),
            pltpu.VMEM((HD, LEN), BF16),
            pltpu.VMEM((REST, HD), BF16),
            pltpu.VMEM((BIG, BIG), F32),
            pltpu.VMEM((REST, REST), F32),
            pltpu.VMEM((LEN, HD), F32),
            spread, spread, spread, spread,
            pltpu.VMEM((HD, LEN), F32),
            pltpu.VMEM((HD, LEN), F32),
            pltpu.VMEM((rounds + 1, 8, HD), F32),
            pltpu.VMEM((rounds + 1, 8, HD), F32),
            dma((4,)), dma((4,)), dma((4,)), dma((4,)), dma((4,)), dma((4,)),
            dma((rounds + 1,)), dma((rounds + 1,)), pltpu.SemaphoreType.REGULAR((rounds + 1,)), dma((4,)),
        ],
        compiler_params=pltpu.CompilerParams(
            collective_id=0, has_side_effects=True, vmem_limit_bytes=48 * 2**20
        ),
    )(*(pltpu.with_memory_space_constraint(x, pltpu.HBM) for x in operands))
    return pl.pallas_call(
        settle,
        out_shape=(rows, rows, rows, rows, gain, gain),
        in_specs=[vmem] * 6,
        out_specs=(hbm,) * 6,
        scratch_shapes=[dma((6,))],
    )(*(pltpu.with_memory_space_constraint(x, pltpu.VMEM) for x in results))


def solution(mesh):
    placed = (
        P("dp", "seq", None),
        P("dp", "seq", None),
        P("dp", "seq", None),
        P("dp", "seq", None),
        P("dp", None),
        P("seq", None),
        P("seq", None),
    )
    return jax.shard_map(
        functools.partial(on_device, mesh.shape["dp"]),
        mesh=mesh,
        in_specs=placed,
        out_specs=(
            P("dp", "seq", None),
            P("dp", "seq", None),
            P("dp", "seq", None),
            P("dp", "seq", None),
            P("seq", None),
            P("seq", None),
        ),
        check_vma=False,
    )
```

```python
import functools
import math

import jax
import jax.numpy as jnp
from jax import lax
from jax.experimental import pallas as pl
from jax.experimental.pallas import tpu as pltpu
from jax.sharding import PartitionSpec as P

MESH = pl.DeviceIdType.MESH
EPSILON = 1e-06
NEGATIVE = -1e30
HD = 128
LEN = 2048
BIG = 1536
REST = LEN - BIG
ROWS = 256
SIDE = 4
SHARDS = SIDE * SIDE
TOK = LEN // SHARDS
GROUP = TOK * SIDE
SCALE = 1.0 / math.sqrt(HD)
EXP2_SCALE = SCALE * math.log2(math.e)
F32 = jnp.float32
BF16 = jnp.bfloat16


def dot_nt(a, b):
    return lax.dot_general(a, b, (((1,), (1,)), ((), ())), preferred_element_type=F32)


def dot_nn(a, b):
    return jnp.dot(a, b, preferred_element_type=F32)


def rows_at(start, size):
    return pl.ds(pl.multiple_of(start, size), size)


def kernel(
    dp_size,
    q_in, k_in, v_in, g_in, seg_in, gain_q_in, gain_k_in,
    o_out, dq_out, dk_out, dv_out, ggq_out, ggk_out,
    seg_s, seg_v, gain_q, gain_k, rx, tx, shifted, units, inverses, qr, kr, vr, gr, q_t, g_t, marks, p_big, p_rest, low_big, low_rest, scale_of,
    go, gq, gk, gv, dk_t, dv_t, gains, gain_rx,
    in_send, in_recv, in_local, out_send, out_recv, out_local, gain_send, gain_recv, ready, small,
):
    d = lax.axis_index("dp")
    me = lax.axis_index("seq")
    mx, my = me // SIDE, me % SIDE
    rounds = dp_size.bit_length() - 1

    def peer(j):
        return (mx + j // SIDE) % SIDE * SIDE + (my + j % SIDE) % SIDE

    def upper(r):
        return (d // (1 << r)) % 2

    def partner(r):
        return d + (1 << r) - 2 * (1 << r) * upper(r)

    barrier = pltpu.get_barrier_semaphore()

    def greet(j, carry):
        pl.semaphore_signal(barrier, inc=1, device_id=(d, peer(j)), device_id_type=MESH)
        return carry

    for r in range(rounds):

        @pl.when(upper(r) == 0)
        def _(r=r):
            pl.semaphore_signal(barrier, inc=1, device_id=(partner(r), me), device_id_type=MESH)

    lax.fori_loop(1, SHARDS, greet, 0)
    pl.semaphore_wait(barrier, SHARDS - 1 + sum(upper(r) for r in range(rounds)))

    sources = (q_in, k_in, v_in, g_in)
    targets = (o_out, dq_out, dk_out, dv_out)
    for a in range(4):

        def send(j, carry, a=a):
            to = peer(j)
            pltpu.make_async_remote_copy(
                src_ref=sources[a].at[0, :, rows_at(to * HD, HD)],
                dst_ref=rx.at[a, rows_at(me * TOK, TOK)],
                send_sem=in_send.at[a],
                recv_sem=in_recv.at[a],
                device_id=(d, to),
                device_id_type=MESH,
            ).start()
            return carry

        lax.fori_loop(1, SHARDS, send, 0)
        pltpu.make_async_copy(
            sources[a].at[0, :, rows_at(me * HD, HD)], rx.at[a, rows_at(me * TOK, TOK)], in_local.at[a]
        ).start()

    for r in range(rounds):

        @pl.when(upper(r) == 1)
        def _(r=r):
            pl.semaphore_signal(ready.at[r], inc=1, device_id=(partner(r), me), device_id_type=MESH)

    fetches = [
        pltpu.make_async_copy(here, there, small.at[i])
        for i, (here, there) in enumerate(
            ((seg_in, seg_s), (seg_in, seg_v), (gain_q_in, gain_q), (gain_k_in, gain_k))
        )
    ]
    for fetch in fetches:
        fetch.start()
    for fetch in fetches:
        fetch.wait()

    image = seg_s[0, LEN // 2]

    def halve(_, held):
        low, high = held
        mid = (low + high) // 2
        inside = seg_s[0, mid] >= image
        return (jnp.where(inside, low, mid + 1), jnp.where(inside, mid, high))

    first, _ = lax.fori_loop(0, 10, halve, (jnp.int32(0), jnp.int32(REST)))

    lanes = lax.broadcasted_iota(jnp.int32, (TOK, HD), 1).astype(F32)
    for t in range(2 * REST // TOK):
        token = (BIG + t * TOK) % LEN
        numbers = seg_v[0:1, token : token + TOK].astype(F32)
        column = jnp.broadcast_to(numbers, (HD, TOK)).T
        shifted[t * TOK : (t + 1) * TOK] = jnp.where(column == lanes, 1.0, 0.0)
    marks[...] = shifted[pl.ds(first, REST), :].astype(BF16)
    gains[0] = jnp.zeros((8, HD), F32)

    def fill(a, gain):
        part = rx.at[a, pl.ds(0, LEN - TOK)]
        pltpu.make_async_copy(part, part, in_recv.at[a]).wait()
        own = rx.at[a, pl.ds(0, TOK)]
        pltpu.make_async_copy(own, own, in_local.at[a]).wait()
        for g in range(SIDE):
            at = pl.ds(g * GROUP, GROUP)
            x = rx[a, at, :].astype(F32)
            if gain is not None:
                inverse = lax.rsqrt(jnp.mean(x * x, axis=1, keepdims=True) + EPSILON)
                x = x * inverse
                units[a, at, :] = x
                inverses[a, at, :] = jnp.broadcast_to(inverse, (GROUP, HD))
                x = x * gain[...]
            shifted[at, :] = x
        shifted[LEN : LEN + REST] = shifted[0:REST]

    def roll_into(rolled, turned):

        def body(b, carry):
            value = shifted[pl.ds(first + b * GROUP, GROUP), :]
            rolled[rows_at(b * GROUP, GROUP), :] = value.astype(BF16)
            if turned is not None:
                turned[:, rows_at(b * GROUP, GROUP)] = value.T.astype(BF16)
            return carry

        lax.fori_loop(0, LEN // GROUP, body, 0)

    fill(0, gain_q)
    roll_into(qr, q_t)
    fill(1, gain_k)
    roll_into(kr, None)

    def powers_of(scores, at):
        top = jnp.max(scores, axis=1, keepdims=True)
        powers = jnp.exp2((scores - top) * EXP2_SCALE)
        scale_of[at, :] = jnp.broadcast_to(1.0 / jnp.sum(powers, axis=1, keepdims=True), (ROWS, HD))
        return powers

    def big_powers(b, carry):
        at = rows_at(b * ROWS, ROWS)
        p_big[at, :] = powers_of(dot_nt(qr[at, :], kr[0:BIG, :]), at)
        return carry

    lax.fori_loop(0, BIG // ROWS, big_powers, 0, unroll=2)

    def rest_powers(b, carry):
        at = rows_at(b * ROWS, ROWS)
        rolled_at = rows_at(BIG + b * ROWS, ROWS)
        scores = dot_nt(qr[rolled_at, :], kr[BIG:LEN, :])
        allowed = dot_nt(marks[at, :], marks[...]) > 0.5
        p_rest[at, :] = powers_of(jnp.where(allowed, scores, NEGATIVE), rolled_at)
        return carry

    lax.fori_loop(0, REST // ROWS, rest_powers, 0, unroll=2)

    fill(2, None)
    roll_into(vr, None)

    def big_values(b, carry):
        at = rows_at(b * ROWS, ROWS)
        low = (p_big[at, :] * scale_of[at, 0:1]).astype(BF16)
        low_big[at, :] = low
        go[rows_at(REST + b * ROWS, ROWS), :] = dot_nn(low, vr[0:BIG, :])
        return carry

    lax.fori_loop(0, BIG // ROWS, big_values, 0, unroll=2)

    def rest_values(b, carry):
        at = rows_at(b * ROWS, ROWS)
        low = (p_rest[at, :] * scale_of[rows_at(BIG + b * ROWS, ROWS), 0:1]).astype(BF16)
        low_rest[at, :] = low
        value = dot_nn(low, vr[BIG:LEN, :])
        go[rows_at(LEN + b * ROWS, ROWS), :] = value
        go[at, :] = value
        return carry

    lax.fori_loop(0, REST // ROWS, rest_values, 0, unroll=2)

    def send_back(a):
        target = targets[a].at[0, :, rows_at(me * HD, HD)]

        def send(j, carry):
            to = peer(j)
            pltpu.make_async_remote_copy(
                src_ref=tx.at[a, rows_at(to * TOK, TOK)],
                dst_ref=target,
                send_sem=out_send.at[a],
                recv_sem=out_recv.at[a],
                device_id=(d, to),
                device_id_type=MESH,
            ).start()
            return carry

        lax.fori_loop(1, SHARDS, send, 0)
        pltpu.make_async_copy(tx.at[a, rows_at(me * TOK, TOK)], target, out_local.at[a]).start()

    def token_group(ref, g):
        return ref[pl.ds(REST - first + g * GROUP, GROUP), :]

    def send_plain(a, ref):
        for g in range(SIDE):
            tx[a, g * GROUP : (g + 1) * GROUP, :] = token_group(ref, g).astype(BF16)
        send_back(a)

    send_plain(0, go)

    fill(3, None)
    roll_into(gr, g_t)

    def head(ref):
        ref[0:REST] = ref[LEN : LEN + REST]

    def columns_of(turned, rows_t):

        def body(c, carry):
            at = rows_at(c * GROUP, GROUP)
            turned[:, at] = dot_nn(rows_t[:, 0:BIG], low_big[:, at])
            return carry

        lax.fori_loop(0, BIG // GROUP, body, 0)
        turned[:, BIG:LEN] = dot_nn(rows_t[:, BIG:LEN], low_rest[...])

    def turn_back(ref, turned, factor):

        def body(b, carry):
            value = turned[:, rows_at(b * GROUP, GROUP)].T
            ref[rows_at(REST + b * GROUP, GROUP), :] = value if factor is None else value * factor
            return carry

        lax.fori_loop(0, LEN // GROUP, body, 0)
        head(ref)

    columns_of(dv_t, g_t)
    turn_back(gv, dv_t, None)
    send_plain(3, gv)

    def backward(powers, queries_at, keys_at, out_at):
        weights = powers * scale_of[queries_at, 0:1]
        grads = gr[queries_at, :]
        delta = jnp.sum(grads.astype(F32) * go[out_at, :], axis=1, keepdims=True)
        grad_probs = dot_nt(grads, vr[keys_at, :])
        grad_scores = (weights * (grad_probs - delta)).astype(BF16)
        gq[out_at, :] = dot_nn(grad_scores, kr[keys_at, :]) * SCALE
        return grad_scores

    def rest_backward(b, carry):
        at = rows_at(b * ROWS, ROWS)
        low_rest[at, :] = backward(
            p_rest[at, :], rows_at(BIG + b * ROWS, ROWS), pl.ds(BIG, REST), rows_at(LEN + b * ROWS, ROWS)
        )
        return carry

    lax.fori_loop(0, REST // ROWS, rest_backward, 0, unroll=2)

    def big_backward(b, carry):
        at = rows_at(b * ROWS, ROWS)
        low_big[at, :] = backward(p_big[at, :], at, pl.ds(0, BIG), rows_at(REST + b * ROWS, ROWS))
        return carry

    lax.fori_loop(0, BIG // ROWS, big_backward, 0, unroll=2)

    def send_normed(a, source, ref, gain):
        total = jnp.zeros((1, HD), F32)
        for g in range(SIDE):
            at = pl.ds(g * GROUP, GROUP)
            unit = units[source, at, :]
            grad = token_group(ref, g)
            total = total + jnp.sum(grad * unit, axis=0, keepdims=True)
            scaled = grad * gain[...]
            inner = jnp.mean(scaled * unit, axis=1, keepdims=True)
            tx[a, at, :] = (inverses[source, at, :] * (scaled - unit * inner)).astype(BF16)
        send_back(a)
        return total

    head(gq)
    gains[0, 0:1, :] = send_normed(1, 0, gq, gain_q)
    columns_of(dk_t, q_t)
    turn_back(gk, dk_t, SCALE)
    gains[0, 1:2, :] = send_normed(2, 1, gk, gain_k)

    for r in range(rounds):

        @pl.when(upper(r) == 0)
        def _(r=r):
            pl.semaphore_wait(ready.at[r], 1)

        copy = pltpu.make_async_remote_copy(
            src_ref=gains.at[r],
            dst_ref=gain_rx.at[r],
            send_sem=gain_send.at[r],
            recv_sem=gain_recv.at[r],
            device_id=(partner(r), me),
            device_id_type=MESH,
        )
        copy.start()
        copy.wait()
        gains[r + 1] = gains[r] + gain_rx[r]
    ggq_out[...] = gains[rounds, 0:1, :]
    ggk_out[...] = gains[rounds, 1:2, :]

    for a in range(4):
        part = rx.at[a, pl.ds(0, LEN - TOK)]
        pltpu.make_async_copy(part, part, in_send.at[a]).wait()
        pltpu.make_async_copy(part, part, out_send.at[a]).wait()
        own = rx.at[a, pl.ds(0, TOK)]
        pltpu.make_async_copy(own, own, out_local.at[a]).wait()
        landed = targets[a].at[0, :, pl.ds(0, LEN - TOK)]
        pltpu.make_async_copy(landed, landed, out_recv.at[a]).wait()


def settle(*refs):
    held, placed, sem = refs[:6], refs[6:12], refs[12]
    copies = [pltpu.make_async_copy(held[i], placed[i], sem.at[i]) for i in range(6)]
    for copy in copies:
        copy.start()
    for copy in copies:
        copy.wait()


def on_device(dp_size, *operands):
    rounds = dp_size.bit_length() - 1
    rows = jax.ShapeDtypeStruct((1, TOK, LEN), BF16)
    gain = jax.ShapeDtypeStruct((1, HD), F32)
    hbm = pl.BlockSpec(memory_space=pltpu.HBM)
    vmem = pl.BlockSpec(memory_space=pltpu.VMEM)
    place = pl.BlockSpec(memory_space=pl.ANY)
    dma = pltpu.SemaphoreType.DMA
    spread = pltpu.VMEM((LEN + REST, HD), F32)
    packed = pltpu.VMEM((LEN, HD), BF16)
    results = pl.pallas_call(
        functools.partial(kernel, dp_size),
        out_shape=(rows, rows, rows, rows, gain, gain),
        in_specs=[hbm] * 7,
        out_specs=(place, place, place, place, vmem, vmem),
        scratch_shapes=[
            pltpu.SMEM((1, LEN), jnp.int32),
            pltpu.VMEM((1, LEN), jnp.int32),
            pltpu.VMEM((1, HD), F32),
            pltpu.VMEM((1, HD), F32),
            pltpu.VMEM((4, LEN, HD), BF16),
            pltpu.VMEM((4, LEN, HD), BF16),
            spread,
            pltpu.VMEM((2, LEN, HD), F32),
            pltpu.VMEM((2, LEN, HD), F32),
            packed, packed, packed, packed,
            pltpu.VMEM((HD, LEN), BF16),
            pltpu.VMEM((HD, LEN), BF16),
            pltpu.VMEM((REST, HD), BF16),
            pltpu.VMEM((BIG, BIG), F32),
            pltpu.VMEM((REST, REST), F32),
            pltpu.VMEM((BIG, BIG), BF16),
            pltpu.VMEM((REST, REST), BF16),
            pltpu.VMEM((LEN, HD), F32),
            spread, spread, spread, spread,
            pltpu.VMEM((HD, LEN), F32),
            pltpu.VMEM((HD, LEN), F32),
            pltpu.VMEM((rounds + 1, 8, HD), F32),
            pltpu.VMEM((rounds + 1, 8, HD), F32),
            dma((4,)), dma((4,)), dma((4,)), dma((4,)), dma((4,)), dma((4,)),
            dma((rounds + 1,)), dma((rounds + 1,)), pltpu.SemaphoreType.REGULAR((rounds + 1,)), dma((4,)),
        ],
        compiler_params=pltpu.CompilerParams(
            collective_id=0, has_side_effects=True, vmem_limit_bytes=48 * 2**20
        ),
    )(*(pltpu.with_memory_space_constraint(x, pltpu.HBM) for x in operands))
    return pl.pallas_call(
        settle,
        out_shape=(rows, rows, rows, rows, gain, gain),
        in_specs=[vmem] * 6,
        out_specs=(hbm,) * 6,
        scratch_shapes=[dma((6,))],
    )(*(pltpu.with_memory_space_constraint(x, pltpu.VMEM) for x in results))


def solution(mesh):
    placed = (
        P("dp", "seq", None),
        P("dp", "seq", None),
        P("dp", "seq", None),
        P("dp", "seq", None),
        P("dp", None),
        P("seq", None),
        P("seq", None),
    )
    return jax.shard_map(
        functools.partial(on_device, mesh.shape["dp"]),
        mesh=mesh,
        in_specs=placed,
        out_specs=(
            P("dp", "seq", None),
            P("dp", "seq", None),
            P("dp", "seq", None),
            P("dp", "seq", None),
            P("seq", None),
            P("seq", None),
        ),
        check_vma=False,
    )
```

```python
import functools
import math

import jax
import jax.numpy as jnp
from jax import lax
from jax.experimental import pallas as pl
from jax.experimental.pallas import tpu as pltpu
from jax.sharding import PartitionSpec as P

MESH = pl.DeviceIdType.MESH
EPSILON = 1e-06
NEGATIVE = -1e30
HD = 128
LEN = 2048
BIG = 1536
REST = LEN - BIG
ROWS = 256
SIDE = 4
SHARDS = SIDE * SIDE
TOK = LEN // SHARDS
GROUP = TOK * SIDE
SCALE = 1.0 / math.sqrt(HD)
EXP2_SCALE = SCALE * math.log2(math.e)
F32 = jnp.float32
BF16 = jnp.bfloat16


def dot_nt(a, b):
    return lax.dot_general(a, b, (((1,), (1,)), ((), ())), preferred_element_type=F32)


def dot_nn(a, b):
    return jnp.dot(a, b, preferred_element_type=F32)


def rows_at(start, size):
    return pl.ds(pl.multiple_of(start, size), size)


def kernel(
    dp_size,
    q_in, k_in, v_in, g_in, seg_in, gain_q_in, gain_k_in,
    o_out, dq_out, dk_out, dv_out, ggq_out, ggk_out,
    seg_s, seg_v, gain_q, gain_k, rx, tx, shifted, units, inverses, qr, kr, vr, gr, q_t, g_t, marks, p_big, p_rest, low_big, low_rest, scale_of,
    go, gq, gk, gv, dk_t, dv_t, gains, gain_rx,
    in_send, in_recv, in_local, out_send, out_recv, out_local, gain_send, gain_recv, ready, small,
):
    d = lax.axis_index("dp")
    me = lax.axis_index("seq")
    mx, my = me // SIDE, me % SIDE
    rounds = dp_size.bit_length() - 1

    def peer(j):
        return (mx + j // SIDE) % SIDE * SIDE + (my + j % SIDE) % SIDE

    def upper(r):
        return (d // (1 << r)) % 2

    def partner(r):
        return d + (1 << r) - 2 * (1 << r) * upper(r)

    barrier = pltpu.get_barrier_semaphore()

    def greet(j, carry):
        pl.semaphore_signal(barrier, inc=1, device_id=(d, peer(j)), device_id_type=MESH)
        return carry

    for r in range(rounds):

        @pl.when(upper(r) == 0)
        def _(r=r):
            pl.semaphore_signal(barrier, inc=1, device_id=(partner(r), me), device_id_type=MESH)

    lax.fori_loop(1, SHARDS, greet, 0)
    pl.semaphore_wait(barrier, SHARDS - 1 + sum(upper(r) for r in range(rounds)))

    sources = (q_in, k_in, v_in, g_in)
    targets = (o_out, dq_out, dk_out, dv_out)
    for a in range(4):

        def send(j, carry, a=a):
            to = peer(j)
            pltpu.make_async_remote_copy(
                src_ref=sources[a].at[0, :, rows_at(to * HD, HD)],
                dst_ref=rx.at[a, rows_at(me * TOK, TOK)],
                send_sem=in_send.at[a],
                recv_sem=in_recv.at[a],
                device_id=(d, to),
                device_id_type=MESH,
            ).start()
            return carry

        lax.fori_loop(1, SHARDS, send, 0)
        pltpu.make_async_copy(
            sources[a].at[0, :, rows_at(me * HD, HD)], rx.at[a, rows_at(me * TOK, TOK)], in_local.at[a]
        ).start()

    for r in range(rounds):

        @pl.when(upper(r) == 1)
        def _(r=r):
            pl.semaphore_signal(ready.at[r], inc=1, device_id=(partner(r), me), device_id_type=MESH)

    fetches = [
        pltpu.make_async_copy(here, there, small.at[i])
        for i, (here, there) in enumerate(
            ((seg_in, seg_s), (seg_in, seg_v), (gain_q_in, gain_q), (gain_k_in, gain_k))
        )
    ]
    for fetch in fetches:
        fetch.start()
    for fetch in fetches:
        fetch.wait()

    image = seg_s[0, LEN // 2]

    def halve(_, held):
        low, high = held
        mid = (low + high) // 2
        inside = seg_s[0, mid] >= image
        return (jnp.where(inside, low, mid + 1), jnp.where(inside, mid, high))

    first, _ = lax.fori_loop(0, 10, halve, (jnp.int32(0), jnp.int32(REST)))

    lanes = lax.broadcasted_iota(jnp.int32, (TOK, HD), 1).astype(F32)
    for t in range(2 * REST // TOK):
        token = (BIG + t * TOK) % LEN
        numbers = seg_v[0:1, token : token + TOK].astype(F32)
        column = jnp.broadcast_to(numbers, (HD, TOK)).T
        shifted[t * TOK : (t + 1) * TOK] = jnp.where(column == lanes, 1.0, 0.0)
    marks[...] = shifted[pl.ds(first, REST), :].astype(BF16)
    gains[0] = jnp.zeros((8, HD), F32)

    def fill(a, gain):
        part = rx.at[a, pl.ds(0, LEN - TOK)]
        pltpu.make_async_copy(part, part, in_recv.at[a]).wait()
        own = rx.at[a, pl.ds(0, TOK)]
        pltpu.make_async_copy(own, own, in_local.at[a]).wait()
        for g in range(SIDE):
            at = pl.ds(g * GROUP, GROUP)
            x = rx[a, at, :].astype(F32)
            if gain is not None:
                inverse = lax.rsqrt(jnp.mean(x * x, axis=1, keepdims=True) + EPSILON)
                x = x * inverse
                units[a, at, :] = x
                inverses[a, at, :] = jnp.broadcast_to(inverse, (GROUP, HD))
                x = x * gain[...]
            shifted[at, :] = x
        shifted[LEN : LEN + REST] = shifted[0:REST]

    def roll_into(rolled, turned):

        def body(b, carry):
            value = shifted[pl.ds(first + b * GROUP, GROUP), :]
            rolled[rows_at(b * GROUP, GROUP), :] = value.astype(BF16)
            if turned is not None:
                turned[:, rows_at(b * GROUP, GROUP)] = value.T.astype(BF16)
            return carry

        lax.fori_loop(0, LEN // GROUP, body, 0, unroll=True)

    fill(0, gain_q)
    roll_into(qr, q_t)
    fill(1, gain_k)
    roll_into(kr, None)

    def powers_of(scores, at):
        top = jnp.max(scores, axis=1, keepdims=True)
        powers = jnp.exp2((scores - top) * EXP2_SCALE)
        scale_of[at, :] = jnp.broadcast_to(1.0 / jnp.sum(powers, axis=1, keepdims=True), (ROWS, HD))
        return powers

    def big_powers(b, carry):
        at = rows_at(b * ROWS, ROWS)
        p_big[at, :] = powers_of(dot_nt(qr[at, :], kr[0:BIG, :]), at)
        return carry

    lax.fori_loop(0, BIG // ROWS, big_powers, 0, unroll=2)

    def rest_powers(b, carry):
        at = rows_at(b * ROWS, ROWS)
        rolled_at = rows_at(BIG + b * ROWS, ROWS)
        scores = dot_nt(qr[rolled_at, :], kr[BIG:LEN, :])
        allowed = dot_nt(marks[at, :], marks[...]) > 0.5
        p_rest[at, :] = powers_of(jnp.where(allowed, scores, NEGATIVE), rolled_at)
        return carry

    lax.fori_loop(0, REST // ROWS, rest_powers, 0, unroll=2)

    fill(2, None)
    roll_into(vr, None)

    def big_values(b, carry):
        at = rows_at(b * ROWS, ROWS)
        low = (p_big[at, :] * scale_of[at, 0:1]).astype(BF16)
        low_big[at, :] = low
        go[rows_at(REST + b * ROWS, ROWS), :] = dot_nn(low, vr[0:BIG, :])
        return carry

    lax.fori_loop(0, BIG // ROWS, big_values, 0, unroll=2)

    def rest_values(b, carry):
        at = rows_at(b * ROWS, ROWS)
        low = (p_rest[at, :] * scale_of[rows_at(BIG + b * ROWS, ROWS), 0:1]).astype(BF16)
        low_rest[at, :] = low
        value = dot_nn(low, vr[BIG:LEN, :])
        go[rows_at(LEN + b * ROWS, ROWS), :] = value
        go[at, :] = value
        return carry

    lax.fori_loop(0, REST // ROWS, rest_values, 0, unroll=2)

    def send_back(a):
        target = targets[a].at[0, :, rows_at(me * HD, HD)]

        def send(j, carry):
            to = peer(j)
            pltpu.make_async_remote_copy(
                src_ref=tx.at[a, rows_at(to * TOK, TOK)],
                dst_ref=target,
                send_sem=out_send.at[a],
                recv_sem=out_recv.at[a],
                device_id=(d, to),
                device_id_type=MESH,
            ).start()
            return carry

        lax.fori_loop(1, SHARDS, send, 0)
        pltpu.make_async_copy(tx.at[a, rows_at(me * TOK, TOK)], target, out_local.at[a]).start()

    def token_group(ref, g):
        return ref[pl.ds(REST - first + g * GROUP, GROUP), :]

    def send_plain(a, ref):
        for g in range(SIDE):
            tx[a, g * GROUP : (g + 1) * GROUP, :] = token_group(ref, g).astype(BF16)
        send_back(a)

    send_plain(0, go)

    fill(3, None)
    roll_into(gr, g_t)

    def head(ref):
        ref[0:REST] = ref[LEN : LEN + REST]

    def columns_of(turned, rows_t):

        def body(c, carry):
            at = rows_at(c * GROUP, GROUP)
            turned[:, at] = dot_nn(rows_t[:, 0:BIG], low_big[:, at])
            return carry

        lax.fori_loop(0, BIG // GROUP, body, 0, unroll=True)
        turned[:, BIG:LEN] = dot_nn(rows_t[:, BIG:LEN], low_rest[...])

    def turn_back(ref, turned, factor):

        def body(b, carry):
            value = turned[:, rows_at(b * GROUP, GROUP)].T
            ref[rows_at(REST + b * GROUP, GROUP), :] = value if factor is None else value * factor
            return carry

        lax.fori_loop(0, LEN // GROUP, body, 0, unroll=True)
        head(ref)

    columns_of(dv_t, g_t)
    turn_back(gv, dv_t, None)
    send_plain(3, gv)

    def backward(powers, queries_at, keys_at, out_at):
        weights = powers * scale_of[queries_at, 0:1]
        grads = gr[queries_at, :]
        delta = jnp.sum(grads.astype(F32) * go[out_at, :], axis=1, keepdims=True)
        grad_probs = dot_nt(grads, vr[keys_at, :])
        grad_scores = (weights * (grad_probs - delta)).astype(BF16)
        gq[out_at, :] = dot_nn(grad_scores, kr[keys_at, :]) * SCALE
        return grad_scores

    def rest_backward(b, carry):
        at = rows_at(b * ROWS, ROWS)
        low_rest[at, :] = backward(
            p_rest[at, :], rows_at(BIG + b * ROWS, ROWS), pl.ds(BIG, REST), rows_at(LEN + b * ROWS, ROWS)
        )
        return carry

    lax.fori_loop(0, REST // ROWS, rest_backward, 0, unroll=2)

    def big_backward(b, carry):
        at = rows_at(b * ROWS, ROWS)
        low_big[at, :] = backward(p_big[at, :], at, pl.ds(0, BIG), rows_at(REST + b * ROWS, ROWS))
        return carry

    lax.fori_loop(0, BIG // ROWS, big_backward, 0, unroll=2)

    def send_normed(a, source, ref, gain):
        total = jnp.zeros((1, HD), F32)
        for g in range(SIDE):
            at = pl.ds(g * GROUP, GROUP)
            unit = units[source, at, :]
            grad = token_group(ref, g)
            total = total + jnp.sum(grad * unit, axis=0, keepdims=True)
            scaled = grad * gain[...]
            inner = jnp.mean(scaled * unit, axis=1, keepdims=True)
            tx[a, at, :] = (inverses[source, at, :] * (scaled - unit * inner)).astype(BF16)
        send_back(a)
        return total

    head(gq)
    gains[0, 0:1, :] = send_normed(1, 0, gq, gain_q)
    columns_of(dk_t, q_t)
    turn_back(gk, dk_t, SCALE)
    gains[0, 1:2, :] = send_normed(2, 1, gk, gain_k)

    for r in range(rounds):

        @pl.when(upper(r) == 0)
        def _(r=r):
            pl.semaphore_wait(ready.at[r], 1)

        copy = pltpu.make_async_remote_copy(
            src_ref=gains.at[r],
            dst_ref=gain_rx.at[r],
            send_sem=gain_send.at[r],
            recv_sem=gain_recv.at[r],
            device_id=(partner(r), me),
            device_id_type=MESH,
        )
        copy.start()
        copy.wait()
        gains[r + 1] = gains[r] + gain_rx[r]
    ggq_out[...] = gains[rounds, 0:1, :]
    ggk_out[...] = gains[rounds, 1:2, :]

    for a in range(4):
        part = rx.at[a, pl.ds(0, LEN - TOK)]
        pltpu.make_async_copy(part, part, in_send.at[a]).wait()
        pltpu.make_async_copy(part, part, out_send.at[a]).wait()
        own = rx.at[a, pl.ds(0, TOK)]
        pltpu.make_async_copy(own, own, out_local.at[a]).wait()
        landed = targets[a].at[0, :, pl.ds(0, LEN - TOK)]
        pltpu.make_async_copy(landed, landed, out_recv.at[a]).wait()


def settle(*refs):
    held, placed, sem = refs[:6], refs[6:12], refs[12]
    copies = [pltpu.make_async_copy(held[i], placed[i], sem.at[i]) for i in range(6)]
    for copy in copies:
        copy.start()
    for copy in copies:
        copy.wait()


def on_device(dp_size, *operands):
    rounds = dp_size.bit_length() - 1
    rows = jax.ShapeDtypeStruct((1, TOK, LEN), BF16)
    gain = jax.ShapeDtypeStruct((1, HD), F32)
    hbm = pl.BlockSpec(memory_space=pltpu.HBM)
    vmem = pl.BlockSpec(memory_space=pltpu.VMEM)
    place = pl.BlockSpec(memory_space=pl.ANY)
    dma = pltpu.SemaphoreType.DMA
    spread = pltpu.VMEM((LEN + REST, HD), F32)
    packed = pltpu.VMEM((LEN, HD), BF16)
    results = pl.pallas_call(
        functools.partial(kernel, dp_size),
        out_shape=(rows, rows, rows, rows, gain, gain),
        in_specs=[hbm] * 7,
        out_specs=(place, place, place, place, vmem, vmem),
        scratch_shapes=[
            pltpu.SMEM((1, LEN), jnp.int32),
            pltpu.VMEM((1, LEN), jnp.int32),
            pltpu.VMEM((1, HD), F32),
            pltpu.VMEM((1, HD), F32),
            pltpu.VMEM((4, LEN, HD), BF16),
            pltpu.VMEM((4, LEN, HD), BF16),
            spread,
            pltpu.VMEM((2, LEN, HD), F32),
            pltpu.VMEM((2, LEN, HD), F32),
            packed, packed, packed, packed,
            pltpu.VMEM((HD, LEN), BF16),
            pltpu.VMEM((HD, LEN), BF16),
            pltpu.VMEM((REST, HD), BF16),
            pltpu.VMEM((BIG, BIG), F32),
            pltpu.VMEM((REST, REST), F32),
            pltpu.VMEM((BIG, BIG), BF16),
            pltpu.VMEM((REST, REST), BF16),
            pltpu.VMEM((LEN, HD), F32),
            spread, spread, spread, spread,
            pltpu.VMEM((HD, LEN), F32),
            pltpu.VMEM((HD, LEN), F32),
            pltpu.VMEM((rounds + 1, 8, HD), F32),
            pltpu.VMEM((rounds + 1, 8, HD), F32),
            dma((4,)), dma((4,)), dma((4,)), dma((4,)), dma((4,)), dma((4,)),
            dma((rounds + 1,)), dma((rounds + 1,)), pltpu.SemaphoreType.REGULAR((rounds + 1,)), dma((4,)),
        ],
        compiler_params=pltpu.CompilerParams(
            collective_id=0, has_side_effects=True, vmem_limit_bytes=48 * 2**20
        ),
    )(*(pltpu.with_memory_space_constraint(x, pltpu.HBM) for x in operands))
    return pl.pallas_call(
        settle,
        out_shape=(rows, rows, rows, rows, gain, gain),
        in_specs=[vmem] * 6,
        out_specs=(hbm,) * 6,
        scratch_shapes=[dma((6,))],
    )(*(pltpu.with_memory_space_constraint(x, pltpu.VMEM) for x in results))


def solution(mesh):
    placed = (
        P("dp", "seq", None),
        P("dp", "seq", None),
        P("dp", "seq", None),
        P("dp", "seq", None),
        P("dp", None),
        P("seq", None),
        P("seq", None),
    )
    return jax.shard_map(
        functools.partial(on_device, mesh.shape["dp"]),
        mesh=mesh,
        in_specs=placed,
        out_specs=(
            P("dp", "seq", None),
            P("dp", "seq", None),
            P("dp", "seq", None),
            P("dp", "seq", None),
            P("seq", None),
            P("seq", None),
        ),
        check_vma=False,
    )
```

```python
import functools
import math

import jax
import jax.numpy as jnp
from jax import lax
from jax.experimental import pallas as pl
from jax.experimental.pallas import tpu as pltpu
from jax.sharding import PartitionSpec as P

MESH = pl.DeviceIdType.MESH
EPSILON = 1e-06
NEGATIVE = -1e30
HD = 128
LEN = 2048
BIG = 1536
REST = LEN - BIG
ROWS = 256
SIDE = 4
SHARDS = SIDE * SIDE
TOK = LEN // SHARDS
GROUP = TOK * SIDE
SCALE = 1.0 / math.sqrt(HD)
EXP2_SCALE = SCALE * math.log2(math.e)
F32 = jnp.float32
BF16 = jnp.bfloat16


def dot_nt(a, b):
    return lax.dot_general(a, b, (((1,), (1,)), ((), ())), preferred_element_type=F32)


def dot_nn(a, b):
    return jnp.dot(a, b, preferred_element_type=F32)


def rows_at(start, size):
    return pl.ds(pl.multiple_of(start, size), size)


def kernel(
    dp_size,
    q_in, k_in, v_in, g_in, seg_in, gain_q_in, gain_k_in,
    o_out, dq_out, dk_out, dv_out, ggq_out, ggk_out,
    seg_s, seg_v, gain_q, gain_k, rx, tx, shifted, units, inverses, qr, kr, vr, gr, q_t, g_t, marks, p_big, p_rest, low_big, low_rest, scale_of,
    go, gq, gk, gv, dk_t, dv_t, gains, gain_rx,
    in_send, in_recv, in_local, out_send, out_recv, out_local, gain_send, gain_recv, ready, small,
):
    d = lax.axis_index("dp")
    me = lax.axis_index("seq")
    mx, my = me // SIDE, me % SIDE
    rounds = dp_size.bit_length() - 1

    def peer(j):
        return (mx + j // SIDE) % SIDE * SIDE + (my + j % SIDE) % SIDE

    def upper(r):
        return (d // (1 << r)) % 2

    def partner(r):
        return d + (1 << r) - 2 * (1 << r) * upper(r)

    barrier = pltpu.get_barrier_semaphore()

    def greet(j, carry):
        pl.semaphore_signal(barrier, inc=1, device_id=(d, peer(j)), device_id_type=MESH)
        return carry

    for r in range(rounds):

        @pl.when(upper(r) == 0)
        def _(r=r):
            pl.semaphore_signal(barrier, inc=1, device_id=(partner(r), me), device_id_type=MESH)

    lax.fori_loop(1, SHARDS, greet, 0)
    pl.semaphore_wait(barrier, SHARDS - 1 + sum(upper(r) for r in range(rounds)))

    sources = (q_in, k_in, v_in, g_in)
    targets = (o_out, dq_out, dk_out, dv_out)
    for a in range(4):

        def send(j, carry, a=a):
            to = peer(j)
            pltpu.make_async_remote_copy(
                src_ref=sources[a].at[0, :, rows_at(to * HD, HD)],
                dst_ref=rx.at[a, rows_at(me * TOK, TOK)],
                send_sem=in_send.at[a],
                recv_sem=in_recv.at[a],
                device_id=(d, to),
                device_id_type=MESH,
            ).start()
            return carry

        lax.fori_loop(1, SHARDS, send, 0)
        pltpu.make_async_copy(
            sources[a].at[0, :, rows_at(me * HD, HD)], rx.at[a, rows_at(me * TOK, TOK)], in_local.at[a]
        ).start()

    for r in range(rounds):

        @pl.when(upper(r) == 1)
        def _(r=r):
            pl.semaphore_signal(ready.at[r], inc=1, device_id=(partner(r), me), device_id_type=MESH)

    fetches = [
        pltpu.make_async_copy(here, there, small.at[i])
        for i, (here, there) in enumerate(
            ((seg_in, seg_s), (seg_in, seg_v), (gain_q_in, gain_q), (gain_k_in, gain_k))
        )
    ]
    for fetch in fetches:
        fetch.start()
    for fetch in fetches:
        fetch.wait()

    image = seg_s[0, LEN // 2]

    def halve(_, held):
        low, high = held
        mid = (low + high) // 2
        inside = seg_s[0, mid] >= image
        return (jnp.where(inside, low, mid + 1), jnp.where(inside, mid, high))

    first, _ = lax.fori_loop(0, 10, halve, (jnp.int32(0), jnp.int32(REST)))

    lanes = lax.broadcasted_iota(jnp.int32, (TOK, HD), 1).astype(F32)
    for t in range(2 * REST // TOK):
        token = (BIG + t * TOK) % LEN
        numbers = seg_v[0:1, token : token + TOK].astype(F32)
        column = jnp.broadcast_to(numbers, (HD, TOK)).T
        shifted[t * TOK : (t + 1) * TOK] = jnp.where(column == lanes, 1.0, 0.0)
    marks[...] = shifted[pl.ds(first, REST), :].astype(BF16)
    gains[0] = jnp.zeros((8, HD), F32)

    def fill(a, gain):
        part = rx.at[a, pl.ds(0, LEN - TOK)]
        pltpu.make_async_copy(part, part, in_recv.at[a]).wait()
        own = rx.at[a, pl.ds(0, TOK)]
        pltpu.make_async_copy(own, own, in_local.at[a]).wait()
        for g in range(SIDE):
            at = pl.ds(g * GROUP, GROUP)
            x = rx[a, at, :].astype(F32)
            if gain is not None:
                inverse = lax.rsqrt(jnp.mean(x * x, axis=1, keepdims=True) + EPSILON)
                x = x * inverse
                units[a, at, :] = x
                inverses[a, at, :] = jnp.broadcast_to(inverse, (GROUP, HD))
                x = x * gain[...]
            shifted[at, :] = x
        shifted[LEN : LEN + REST] = shifted[0:REST]

    def roll_into(rolled, turned):

        def body(b, carry):
            value = shifted[pl.ds(first + b * GROUP, GROUP), :]
            rolled[rows_at(b * GROUP, GROUP), :] = value.astype(BF16)
            if turned is not None:
                turned[:, rows_at(b * GROUP, GROUP)] = value.T.astype(BF16)
            return carry

        lax.fori_loop(0, LEN // GROUP, body, 0, unroll=True)

    fill(0, gain_q)
    roll_into(qr, q_t)
    fill(1, gain_k)
    roll_into(kr, None)

    def powers_of(scores, at):
        top = jnp.max(scores, axis=1, keepdims=True)
        powers = jnp.exp2((scores - top) * EXP2_SCALE)
        scale_of[at, :] = jnp.broadcast_to(1.0 / jnp.sum(powers, axis=1, keepdims=True), (ROWS, HD))
        return powers

    def big_powers(b, carry):
        at = rows_at(b * ROWS, ROWS)
        p_big[at, :] = powers_of(dot_nt(qr[at, :], kr[0:BIG, :]), at)
        return carry

    lax.fori_loop(0, BIG // ROWS, big_powers, 0, unroll=2)

    def rest_powers(b, carry):
        at = rows_at(b * ROWS, ROWS)
        rolled_at = rows_at(BIG + b * ROWS, ROWS)
        scores = dot_nt(qr[rolled_at, :], kr[BIG:LEN, :])
        allowed = dot_nt(marks[at, :], marks[...]) > 0.5
        p_rest[at, :] = powers_of(jnp.where(allowed, scores, NEGATIVE), rolled_at)
        return carry

    lax.fori_loop(0, REST // ROWS, rest_powers, 0, unroll=2)

    fill(2, None)
    roll_into(vr, None)

    def big_values(b, carry):
        at = rows_at(b * ROWS, ROWS)
        low = (p_big[at, :] * scale_of[at, 0:1]).astype(BF16)
        low_big[at, :] = low
        go[rows_at(REST + b * ROWS, ROWS), :] = dot_nn(low, vr[0:BIG, :])
        return carry

    lax.fori_loop(0, BIG // ROWS, big_values, 0, unroll=True)

    def rest_values(b, carry):
        at = rows_at(b * ROWS, ROWS)
        low = (p_rest[at, :] * scale_of[rows_at(BIG + b * ROWS, ROWS), 0:1]).astype(BF16)
        low_rest[at, :] = low
        value = dot_nn(low, vr[BIG:LEN, :])
        go[rows_at(LEN + b * ROWS, ROWS), :] = value
        go[at, :] = value
        return carry

    lax.fori_loop(0, REST // ROWS, rest_values, 0, unroll=True)

    def send_back(a):
        target = targets[a].at[0, :, rows_at(me * HD, HD)]

        def send(j, carry):
            to = peer(j)
            pltpu.make_async_remote_copy(
                src_ref=tx.at[a, rows_at(to * TOK, TOK)],
                dst_ref=target,
                send_sem=out_send.at[a],
                recv_sem=out_recv.at[a],
                device_id=(d, to),
                device_id_type=MESH,
            ).start()
            return carry

        lax.fori_loop(1, SHARDS, send, 0)
        pltpu.make_async_copy(tx.at[a, rows_at(me * TOK, TOK)], target, out_local.at[a]).start()

    def token_group(ref, g):
        return ref[pl.ds(REST - first + g * GROUP, GROUP), :]

    def send_plain(a, ref):
        for g in range(SIDE):
            tx[a, g * GROUP : (g + 1) * GROUP, :] = token_group(ref, g).astype(BF16)
        send_back(a)

    send_plain(0, go)

    fill(3, None)
    roll_into(gr, g_t)

    def head(ref):
        ref[0:REST] = ref[LEN : LEN + REST]

    def columns_of(turned, rows_t):

        def body(c, carry):
            at = rows_at(c * GROUP, GROUP)
            turned[:, at] = dot_nn(rows_t[:, 0:BIG], low_big[:, at])
            return carry

        lax.fori_loop(0, BIG // GROUP, body, 0, unroll=True)
        turned[:, BIG:LEN] = dot_nn(rows_t[:, BIG:LEN], low_rest[...])

    def turn_back(ref, turned, factor):

        def body(b, carry):
            value = turned[:, rows_at(b * GROUP, GROUP)].T
            ref[rows_at(REST + b * GROUP, GROUP), :] = value if factor is None else value * factor
            return carry

        lax.fori_loop(0, LEN // GROUP, body, 0, unroll=True)
        head(ref)

    columns_of(dv_t, g_t)
    turn_back(gv, dv_t, None)
    send_plain(3, gv)

    def backward(powers, queries_at, keys_at, out_at):
        weights = powers * scale_of[queries_at, 0:1]
        grads = gr[queries_at, :]
        delta = jnp.sum(grads.astype(F32) * go[out_at, :], axis=1, keepdims=True)
        grad_probs = dot_nt(grads, vr[keys_at, :])
        grad_scores = (weights * (grad_probs - delta)).astype(BF16)
        gq[out_at, :] = dot_nn(grad_scores, kr[keys_at, :]) * SCALE
        return grad_scores

    def rest_backward(b, carry):
        at = rows_at(b * ROWS, ROWS)
        low_rest[at, :] = backward(
            p_rest[at, :], rows_at(BIG + b * ROWS, ROWS), pl.ds(BIG, REST), rows_at(LEN + b * ROWS, ROWS)
        )
        return carry

    lax.fori_loop(0, REST // ROWS, rest_backward, 0, unroll=True)

    def big_backward(b, carry):
        at = rows_at(b * ROWS, ROWS)
        low_big[at, :] = backward(p_big[at, :], at, pl.ds(0, BIG), rows_at(REST + b * ROWS, ROWS))
        return carry

    lax.fori_loop(0, BIG // ROWS, big_backward, 0, unroll=True)

    def send_normed(a, source, ref, gain):
        total = jnp.zeros((1, HD), F32)
        for g in range(SIDE):
            at = pl.ds(g * GROUP, GROUP)
            unit = units[source, at, :]
            grad = token_group(ref, g)
            total = total + jnp.sum(grad * unit, axis=0, keepdims=True)
            scaled = grad * gain[...]
            inner = jnp.mean(scaled * unit, axis=1, keepdims=True)
            tx[a, at, :] = (inverses[source, at, :] * (scaled - unit * inner)).astype(BF16)
        send_back(a)
        return total

    head(gq)
    gains[0, 0:1, :] = send_normed(1, 0, gq, gain_q)
    columns_of(dk_t, q_t)
    turn_back(gk, dk_t, SCALE)
    gains[0, 1:2, :] = send_normed(2, 1, gk, gain_k)

    for r in range(rounds):

        @pl.when(upper(r) == 0)
        def _(r=r):
            pl.semaphore_wait(ready.at[r], 1)

        copy = pltpu.make_async_remote_copy(
            src_ref=gains.at[r],
            dst_ref=gain_rx.at[r],
            send_sem=gain_send.at[r],
            recv_sem=gain_recv.at[r],
            device_id=(partner(r), me),
            device_id_type=MESH,
        )
        copy.start()
        copy.wait()
        gains[r + 1] = gains[r] + gain_rx[r]
    ggq_out[...] = gains[rounds, 0:1, :]
    ggk_out[...] = gains[rounds, 1:2, :]

    for a in range(4):
        part = rx.at[a, pl.ds(0, LEN - TOK)]
        pltpu.make_async_copy(part, part, in_send.at[a]).wait()
        pltpu.make_async_copy(part, part, out_send.at[a]).wait()
        own = rx.at[a, pl.ds(0, TOK)]
        pltpu.make_async_copy(own, own, out_local.at[a]).wait()
        landed = targets[a].at[0, :, pl.ds(0, LEN - TOK)]
        pltpu.make_async_copy(landed, landed, out_recv.at[a]).wait()


def settle(*refs):
    held, placed, sem = refs[:6], refs[6:12], refs[12]
    copies = [pltpu.make_async_copy(held[i], placed[i], sem.at[i]) for i in range(6)]
    for copy in copies:
        copy.start()
    for copy in copies:
        copy.wait()


def on_device(dp_size, *operands):
    rounds = dp_size.bit_length() - 1
    rows = jax.ShapeDtypeStruct((1, TOK, LEN), BF16)
    gain = jax.ShapeDtypeStruct((1, HD), F32)
    hbm = pl.BlockSpec(memory_space=pltpu.HBM)
    vmem = pl.BlockSpec(memory_space=pltpu.VMEM)
    place = pl.BlockSpec(memory_space=pl.ANY)
    dma = pltpu.SemaphoreType.DMA
    spread = pltpu.VMEM((LEN + REST, HD), F32)
    packed = pltpu.VMEM((LEN, HD), BF16)
    results = pl.pallas_call(
        functools.partial(kernel, dp_size),
        out_shape=(rows, rows, rows, rows, gain, gain),
        in_specs=[hbm] * 7,
        out_specs=(place, place, place, place, vmem, vmem),
        scratch_shapes=[
            pltpu.SMEM((1, LEN), jnp.int32),
            pltpu.VMEM((1, LEN), jnp.int32),
            pltpu.VMEM((1, HD), F32),
            pltpu.VMEM((1, HD), F32),
            pltpu.VMEM((4, LEN, HD), BF16),
            pltpu.VMEM((4, LEN, HD), BF16),
            spread,
            pltpu.VMEM((2, LEN, HD), F32),
            pltpu.VMEM((2, LEN, HD), F32),
            packed, packed, packed, packed,
            pltpu.VMEM((HD, LEN), BF16),
            pltpu.VMEM((HD, LEN), BF16),
            pltpu.VMEM((REST, HD), BF16),
            pltpu.VMEM((BIG, BIG), F32),
            pltpu.VMEM((REST, REST), F32),
            pltpu.VMEM((BIG, BIG), BF16),
            pltpu.VMEM((REST, REST), BF16),
            pltpu.VMEM((LEN, HD), F32),
            spread, spread, spread, spread,
            pltpu.VMEM((HD, LEN), F32),
            pltpu.VMEM((HD, LEN), F32),
            pltpu.VMEM((rounds + 1, 8, HD), F32),
            pltpu.VMEM((rounds + 1, 8, HD), F32),
            dma((4,)), dma((4,)), dma((4,)), dma((4,)), dma((4,)), dma((4,)),
            dma((rounds + 1,)), dma((rounds + 1,)), pltpu.SemaphoreType.REGULAR((rounds + 1,)), dma((4,)),
        ],
        compiler_params=pltpu.CompilerParams(
            collective_id=0, has_side_effects=True, vmem_limit_bytes=48 * 2**20
        ),
    )(*(pltpu.with_memory_space_constraint(x, pltpu.HBM) for x in operands))
    return pl.pallas_call(
        settle,
        out_shape=(rows, rows, rows, rows, gain, gain),
        in_specs=[vmem] * 6,
        out_specs=(hbm,) * 6,
        scratch_shapes=[dma((6,))],
    )(*(pltpu.with_memory_space_constraint(x, pltpu.VMEM) for x in results))


def solution(mesh):
    placed = (
        P("dp", "seq", None),
        P("dp", "seq", None),
        P("dp", "seq", None),
        P("dp", "seq", None),
        P("dp", None),
        P("seq", None),
        P("seq", None),
    )
    return jax.shard_map(
        functools.partial(on_device, mesh.shape["dp"]),
        mesh=mesh,
        in_specs=placed,
        out_specs=(
            P("dp", "seq", None),
            P("dp", "seq", None),
            P("dp", "seq", None),
            P("dp", "seq", None),
            P("seq", None),
            P("seq", None),
        ),
        check_vma=False,
    )
```

```python
import functools
import math

import jax
import jax.numpy as jnp
from jax import lax
from jax.experimental import pallas as pl
from jax.experimental.pallas import tpu as pltpu
from jax.sharding import PartitionSpec as P

MESH = pl.DeviceIdType.MESH
EPSILON = 1e-06
NEGATIVE = -1e30
HD = 128
LEN = 2048
BIG = 1536
REST = LEN - BIG
ROWS = 256
SIDE = 4
SHARDS = SIDE * SIDE
TOK = LEN // SHARDS
GROUP = TOK * SIDE
SCALE = 1.0 / math.sqrt(HD)
EXP2_SCALE = SCALE * math.log2(math.e)
F32 = jnp.float32
BF16 = jnp.bfloat16


def dot_nt(a, b):
    return lax.dot_general(a, b, (((1,), (1,)), ((), ())), preferred_element_type=F32)


def dot_nn(a, b):
    return jnp.dot(a, b, preferred_element_type=F32)


def rows_at(start, size):
    return pl.ds(pl.multiple_of(start, size), size)


def kernel(
    dp_size,
    q_in, k_in, v_in, g_in, seg_in, gain_q_in, gain_k_in,
    o_out, dq_out, dk_out, dv_out, ggq_out, ggk_out,
    seg_s, seg_v, gain_q, gain_k, rx, tx, shifted, units, inverses, qr, kr, vr, gr, q_t, g_t, marks, p_big, p_rest, low_big, low_rest, scale_of,
    go, gq, gk, gv, dk_t, dv_t, gains, gain_rx,
    in_send, in_recv, in_local, out_send, out_recv, out_local, gain_send, gain_recv, ready, small,
):
    d = lax.axis_index("dp")
    me = lax.axis_index("seq")
    mx, my = me // SIDE, me % SIDE
    rounds = dp_size.bit_length() - 1

    def peer(j):
        return (mx + j // SIDE) % SIDE * SIDE + (my + j % SIDE) % SIDE

    def upper(r):
        return (d // (1 << r)) % 2

    def partner(r):
        return d + (1 << r) - 2 * (1 << r) * upper(r)

    barrier = pltpu.get_barrier_semaphore()

    def greet(j, carry):
        pl.semaphore_signal(barrier, inc=1, device_id=(d, peer(j)), device_id_type=MESH)
        return carry

    lax.fori_loop(1, SHARDS, greet, 0, unroll=True)

    for r in range(rounds):

        @pl.when(upper(r) == 0)
        def _(r=r):
            pl.semaphore_signal(barrier, inc=1, device_id=(partner(r), me), device_id_type=MESH)

    pl.semaphore_wait(barrier, SHARDS - 1 + sum(upper(r) for r in range(rounds)))

    sources = (q_in, k_in, v_in, g_in)
    targets = (o_out, dq_out, dk_out, dv_out)
    for a in range(4):

        def send(j, carry, a=a):
            to = peer(j)
            pltpu.make_async_remote_copy(
                src_ref=sources[a].at[0, :, rows_at(to * HD, HD)],
                dst_ref=rx.at[a, rows_at(me * TOK, TOK)],
                send_sem=in_send.at[a],
                recv_sem=in_recv.at[a],
                device_id=(d, to),
                device_id_type=MESH,
            ).start()
            return carry

        lax.fori_loop(1, SHARDS, send, 0)
        pltpu.make_async_copy(
            sources[a].at[0, :, rows_at(me * HD, HD)], rx.at[a, rows_at(me * TOK, TOK)], in_local.at[a]
        ).start()

    for r in range(rounds):

        @pl.when(upper(r) == 1)
        def _(r=r):
            pl.semaphore_signal(ready.at[r], inc=1, device_id=(partner(r), me), device_id_type=MESH)

    fetches = [
        pltpu.make_async_copy(here, there, small.at[i])
        for i, (here, there) in enumerate(
            ((seg_in, seg_s), (seg_in, seg_v), (gain_q_in, gain_q), (gain_k_in, gain_k))
        )
    ]
    for fetch in fetches:
        fetch.start()
    for fetch in fetches:
        fetch.wait()

    image = seg_s[0, LEN // 2]

    def halve(_, held):
        low, high = held
        mid = (low + high) // 2
        inside = seg_s[0, mid] >= image
        return (jnp.where(inside, low, mid + 1), jnp.where(inside, mid, high))

    first, _ = lax.fori_loop(0, 10, halve, (jnp.int32(0), jnp.int32(REST)))

    lanes = lax.broadcasted_iota(jnp.int32, (TOK, HD), 1).astype(F32)
    for t in range(2 * REST // TOK):
        token = (BIG + t * TOK) % LEN
        numbers = seg_v[0:1, token : token + TOK].astype(F32)
        column = jnp.broadcast_to(numbers, (HD, TOK)).T
        shifted[t * TOK : (t + 1) * TOK] = jnp.where(column == lanes, 1.0, 0.0)
    marks[...] = shifted[pl.ds(first, REST), :].astype(BF16)
    gains[0] = jnp.zeros((8, HD), F32)

    def fill(a, gain):
        part = rx.at[a, pl.ds(0, LEN - TOK)]
        pltpu.make_async_copy(part, part, in_recv.at[a]).wait()
        own = rx.at[a, pl.ds(0, TOK)]
        pltpu.make_async_copy(own, own, in_local.at[a]).wait()
        for g in range(SIDE):
            at = pl.ds(g * GROUP, GROUP)
            x = rx[a, at, :].astype(F32)
            if gain is not None:
                inverse = lax.rsqrt(jnp.mean(x * x, axis=1, keepdims=True) + EPSILON)
                x = x * inverse
                units[a, at, :] = x
                inverses[a, at, :] = jnp.broadcast_to(inverse, (GROUP, HD))
                x = x * gain[...]
            shifted[at, :] = x
        shifted[LEN : LEN + REST] = shifted[0:REST]

    def roll_into(rolled, turned):

        def body(b, carry):
            value = shifted[pl.ds(first + b * GROUP, GROUP), :]
            rolled[rows_at(b * GROUP, GROUP), :] = value.astype(BF16)
            if turned is not None:
                turned[:, rows_at(b * GROUP, GROUP)] = value.T.astype(BF16)
            return carry

        lax.fori_loop(0, LEN // GROUP, body, 0, unroll=True)

    fill(0, gain_q)
    roll_into(qr, q_t)
    fill(1, gain_k)
    roll_into(kr, None)

    def powers_of(scores, at):
        top = jnp.max(scores, axis=1, keepdims=True)
        powers = jnp.exp2((scores - top) * EXP2_SCALE)
        scale_of[at, :] = jnp.broadcast_to(1.0 / jnp.sum(powers, axis=1, keepdims=True), (ROWS, HD))
        return powers

    def big_powers(b, carry):
        at = rows_at(b * ROWS, ROWS)
        p_big[at, :] = powers_of(dot_nt(qr[at, :], kr[0:BIG, :]), at)
        return carry

    lax.fori_loop(0, BIG // ROWS, big_powers, 0, unroll=2)

    def rest_powers(b, carry):
        at = rows_at(b * ROWS, ROWS)
        rolled_at = rows_at(BIG + b * ROWS, ROWS)
        scores = dot_nt(qr[rolled_at, :], kr[BIG:LEN, :])
        allowed = dot_nt(marks[at, :], marks[...]) > 0.5
        p_rest[at, :] = powers_of(jnp.where(allowed, scores, NEGATIVE), rolled_at)
        return carry

    lax.fori_loop(0, REST // ROWS, rest_powers, 0, unroll=2)

    fill(2, None)
    roll_into(vr, None)

    def big_values(b, carry):
        at = rows_at(b * ROWS, ROWS)
        low = (p_big[at, :] * scale_of[at, 0:1]).astype(BF16)
        low_big[at, :] = low
        go[rows_at(REST + b * ROWS, ROWS), :] = dot_nn(low, vr[0:BIG, :])
        return carry

    lax.fori_loop(0, BIG // ROWS, big_values, 0, unroll=True)

    def rest_values(b, carry):
        at = rows_at(b * ROWS, ROWS)
        low = (p_rest[at, :] * scale_of[rows_at(BIG + b * ROWS, ROWS), 0:1]).astype(BF16)
        low_rest[at, :] = low
        value = dot_nn(low, vr[BIG:LEN, :])
        go[rows_at(LEN + b * ROWS, ROWS), :] = value
        go[at, :] = value
        return carry

    lax.fori_loop(0, REST // ROWS, rest_values, 0, unroll=True)

    def send_back(a):
        target = targets[a].at[0, :, rows_at(me * HD, HD)]

        def send(j, carry):
            to = peer(j)
            pltpu.make_async_remote_copy(
                src_ref=tx.at[a, rows_at(to * TOK, TOK)],
                dst_ref=target,
                send_sem=out_send.at[a],
                recv_sem=out_recv.at[a],
                device_id=(d, to),
                device_id_type=MESH,
            ).start()
            return carry

        lax.fori_loop(1, SHARDS, send, 0)
        pltpu.make_async_copy(tx.at[a, rows_at(me * TOK, TOK)], target, out_local.at[a]).start()

    def token_group(ref, g):
        return ref[pl.ds(REST - first + g * GROUP, GROUP), :]

    def send_plain(a, ref):
        for g in range(SIDE):
            tx[a, g * GROUP : (g + 1) * GROUP, :] = token_group(ref, g).astype(BF16)
        send_back(a)

    send_plain(0, go)

    fill(3, None)
    roll_into(gr, g_t)

    def head(ref):
        ref[0:REST] = ref[LEN : LEN + REST]

    def columns_of(turned, rows_t):

        def body(c, carry):
            at = rows_at(c * GROUP, GROUP)
            turned[:, at] = dot_nn(rows_t[:, 0:BIG], low_big[:, at])
            return carry

        lax.fori_loop(0, BIG // GROUP, body, 0, unroll=True)
        turned[:, BIG:LEN] = dot_nn(rows_t[:, BIG:LEN], low_rest[...])

    def turn_back(ref, turned, factor):

        def body(b, carry):
            value = turned[:, rows_at(b * GROUP, GROUP)].T
            ref[rows_at(REST + b * GROUP, GROUP), :] = value if factor is None else value * factor
            return carry

        lax.fori_loop(0, LEN // GROUP, body, 0, unroll=True)
        head(ref)

    columns_of(dv_t, g_t)
    turn_back(gv, dv_t, None)
    send_plain(3, gv)

    def backward(powers, queries_at, keys_at, out_at):
        weights = powers * scale_of[queries_at, 0:1]
        grads = gr[queries_at, :]
        delta = jnp.sum(grads.astype(F32) * go[out_at, :], axis=1, keepdims=True)
        grad_probs = dot_nt(grads, vr[keys_at, :])
        grad_scores = (weights * (grad_probs - delta)).astype(BF16)
        gq[out_at, :] = dot_nn(grad_scores, kr[keys_at, :]) * SCALE
        return grad_scores

    def rest_backward(b, carry):
        at = rows_at(b * ROWS, ROWS)
        low_rest[at, :] = backward(
            p_rest[at, :], rows_at(BIG + b * ROWS, ROWS), pl.ds(BIG, REST), rows_at(LEN + b * ROWS, ROWS)
        )
        return carry

    lax.fori_loop(0, REST // ROWS, rest_backward, 0, unroll=True)

    def big_backward(b, carry):
        at = rows_at(b * ROWS, ROWS)
        low_big[at, :] = backward(p_big[at, :], at, pl.ds(0, BIG), rows_at(REST + b * ROWS, ROWS))
        return carry

    lax.fori_loop(0, BIG // ROWS, big_backward, 0, unroll=True)

    def send_normed(a, source, ref, gain):
        total = jnp.zeros((1, HD), F32)
        for g in range(SIDE):
            at = pl.ds(g * GROUP, GROUP)
            unit = units[source, at, :]
            grad = token_group(ref, g)
            total = total + jnp.sum(grad * unit, axis=0, keepdims=True)
            scaled = grad * gain[...]
            inner = jnp.mean(scaled * unit, axis=1, keepdims=True)
            tx[a, at, :] = (inverses[source, at, :] * (scaled - unit * inner)).astype(BF16)
        send_back(a)
        return total

    head(gq)
    gains[0, 0:1, :] = send_normed(1, 0, gq, gain_q)
    columns_of(dk_t, q_t)
    turn_back(gk, dk_t, SCALE)
    gains[0, 1:2, :] = send_normed(2, 1, gk, gain_k)

    for r in range(rounds):

        @pl.when(upper(r) == 0)
        def _(r=r):
            pl.semaphore_wait(ready.at[r], 1)

        copy = pltpu.make_async_remote_copy(
            src_ref=gains.at[r],
            dst_ref=gain_rx.at[r],
            send_sem=gain_send.at[r],
            recv_sem=gain_recv.at[r],
            device_id=(partner(r), me),
            device_id_type=MESH,
        )
        copy.start()
        copy.wait()
        gains[r + 1] = gains[r] + gain_rx[r]
    ggq_out[...] = gains[rounds, 0:1, :]
    ggk_out[...] = gains[rounds, 1:2, :]

    for a in range(4):
        part = rx.at[a, pl.ds(0, LEN - TOK)]
        pltpu.make_async_copy(part, part, in_send.at[a]).wait()
        pltpu.make_async_copy(part, part, out_send.at[a]).wait()
        own = rx.at[a, pl.ds(0, TOK)]
        pltpu.make_async_copy(own, own, out_local.at[a]).wait()
        landed = targets[a].at[0, :, pl.ds(0, LEN - TOK)]
        pltpu.make_async_copy(landed, landed, out_recv.at[a]).wait()


def settle(*refs):
    held, placed, sem = refs[:6], refs[6:12], refs[12]
    copies = [pltpu.make_async_copy(held[i], placed[i], sem.at[i]) for i in range(6)]
    for copy in copies:
        copy.start()
    for copy in copies:
        copy.wait()


def on_device(dp_size, *operands):
    rounds = dp_size.bit_length() - 1
    rows = jax.ShapeDtypeStruct((1, TOK, LEN), BF16)
    gain = jax.ShapeDtypeStruct((1, HD), F32)
    hbm = pl.BlockSpec(memory_space=pltpu.HBM)
    vmem = pl.BlockSpec(memory_space=pltpu.VMEM)
    place = pl.BlockSpec(memory_space=pl.ANY)
    dma = pltpu.SemaphoreType.DMA
    spread = pltpu.VMEM((LEN + REST, HD), F32)
    packed = pltpu.VMEM((LEN, HD), BF16)
    results = pl.pallas_call(
        functools.partial(kernel, dp_size),
        out_shape=(rows, rows, rows, rows, gain, gain),
        in_specs=[hbm] * 7,
        out_specs=(place, place, place, place, vmem, vmem),
        scratch_shapes=[
            pltpu.SMEM((1, LEN), jnp.int32),
            pltpu.VMEM((1, LEN), jnp.int32),
            pltpu.VMEM((1, HD), F32),
            pltpu.VMEM((1, HD), F32),
            pltpu.VMEM((4, LEN, HD), BF16),
            pltpu.VMEM((4, LEN, HD), BF16),
            spread,
            pltpu.VMEM((2, LEN, HD), F32),
            pltpu.VMEM((2, LEN, HD), F32),
            packed, packed, packed, packed,
            pltpu.VMEM((HD, LEN), BF16),
            pltpu.VMEM((HD, LEN), BF16),
            pltpu.VMEM((REST, HD), BF16),
            pltpu.VMEM((BIG, BIG), F32),
            pltpu.VMEM((REST, REST), F32),
            pltpu.VMEM((BIG, BIG), BF16),
            pltpu.VMEM((REST, REST), BF16),
            pltpu.VMEM((LEN, HD), F32),
            spread, spread, spread, spread,
            pltpu.VMEM((HD, LEN), F32),
            pltpu.VMEM((HD, LEN), F32),
            pltpu.VMEM((rounds + 1, 8, HD), F32),
            pltpu.VMEM((rounds + 1, 8, HD), F32),
            dma((4,)), dma((4,)), dma((4,)), dma((4,)), dma((4,)), dma((4,)),
            dma((rounds + 1,)), dma((rounds + 1,)), pltpu.SemaphoreType.REGULAR((rounds + 1,)), dma((4,)),
        ],
        compiler_params=pltpu.CompilerParams(
            collective_id=0, has_side_effects=True, vmem_limit_bytes=48 * 2**20
        ),
    )(*(pltpu.with_memory_space_constraint(x, pltpu.HBM) for x in operands))
    return pl.pallas_call(
        settle,
        out_shape=(rows, rows, rows, rows, gain, gain),
        in_specs=[vmem] * 6,
        out_specs=(hbm,) * 6,
        scratch_shapes=[dma((6,))],
    )(*(pltpu.with_memory_space_constraint(x, pltpu.VMEM) for x in results))


def solution(mesh):
    placed = (
        P("dp", "seq", None),
        P("dp", "seq", None),
        P("dp", "seq", None),
        P("dp", "seq", None),
        P("dp", None),
        P("seq", None),
        P("seq", None),
    )
    return jax.shard_map(
        functools.partial(on_device, mesh.shape["dp"]),
        mesh=mesh,
        in_specs=placed,
        out_specs=(
            P("dp", "seq", None),
            P("dp", "seq", None),
            P("dp", "seq", None),
            P("dp", "seq", None),
            P("seq", None),
            P("seq", None),
        ),
        check_vma=False,
    )
```
